32 devices in a mesh: row: 8 (over y, x, core), col: 4 (over z).
Axes of the slice: x: 2, y: 2, z: 4, core: 2. Of those that a mesh axis runs over, the one named last changes fastest.
Arguments:
- pair_map: bfloat16 [256, 256, 128], P('row', 'col'), may hold values from -6 to 6
- token_mask: int32 [256], replicated, may hold values 0 or 1
- norm_gain: float32 [2, 128], replicated, may hold values from 0.1 to 1.9
- norm_bias: float32 [2, 128], replicated, may hold values from -3 to 3
- proj_weight: bfloat16 [2, 128, 256], replicated, may hold values from -0.5 to 0.5
- gate_weight: bfloat16 [2, 128, 256], replicated, may hold values from -0.5 to 0.5
- out_gain: float32 [2, 128], replicated, may hold values from 0.1 to 1.9
- out_bias: float32 [2, 128], replicated, may hold values from -3 to 3
- final_weight: bfloat16 [2, 128, 128], replicated, may hold values from -0.5 to 0.5
- output_gate: bfloat16 [2, 128, 128], replicated, may hold values from -0.5 to 0.5
Outputs:
- updated_pair: bfloat16 [256, 256, 128], P('row', 'col')
The draws below stay inside these ranges and needn't reach their ends.
Inputs may be any that keep to these rules, and one draw needn't show every extreme that they name: `token_mask`: 1 marks a real token, 0 a padding token.
All inputs are finite; a program needn't handle non-finite values.
Results may differ from the reference program's by a relative error of at most 0.014.
Values may be sent and summed in bfloat16 or wider, within the bound.
No kernel may reach another device: no remote copies, remote signals or barrier semaphores. Data moves between devices by JAX's collectives and lax.ppermute only.
A program may use at most 128 MiB of HBM per device.

```python
import jax
import jax.numpy as jnp
from jax import lax

C = 128
H = 128
TOKENS = 256


def with_ends(drawn, stream_key, smallest, high):
    dims = drawn.shape
    place = [jax.random.randint(jax.random.fold_in(stream_key, axis), (), 0, dims[axis]) for axis in range(len(dims))]
    drawn = drawn.at[tuple(place)].set(smallest)
    longest = dims.index(max(dims))
    place[longest] = (place[longest] + 1) % dims[longest]
    return drawn.at[tuple(place)].set(high)


def shard_levels(key, dims, split, smallest, high):
    factor_of, own = 1.0, jax.random.fold_in(key, 6)
    for dim, shards_of in split:
        heights = jnp.exp(jax.random.uniform(jax.random.fold_in(own, dim), (shards_of,), jnp.float32, smallest / len(split), high / len(split)))
        factor_of = factor_of * jnp.repeat(heights, dims[dim] // shards_of).reshape([-1 if axis == dim else 1 for axis in range(len(dims))])
    return factor_of


def normal_values(rng, extent, spread, most, shards=(), kind=jnp.bfloat16):
    array = spread * jax.random.normal(rng, extent, jnp.float32)
    if shards:
        array = array * shard_levels(rng, extent, shards, -0.22, 0.18)
    return jnp.clip(array, -most, most).astype(kind)


def setup_inputs(seed: int = 0) -> dict:
    keys = jax.random.split(jax.random.key(seed), 11)
    return {
        "pair_map": normal_values(keys[0], (TOKENS, TOKENS, C), 1.0, 6.0, ((0, 8), (1, 4))),
        "token_mask": with_ends((jax.random.randint(keys[1], (TOKENS,), 0, 8) < 7).astype(jnp.int32), jax.random.fold_in(keys[1], 1), 0, 1),
        "norm_gain": jnp.clip(1.0 + 0.18 * jax.random.normal(keys[2], (2, C), jnp.float32), 0.1, 1.9),
        "norm_bias": normal_values(keys[3], (2, C), 0.5, 3.0, (), jnp.float32),
        "proj_weight": normal_values(keys[4], (2, C, 2 * H), C ** -0.5, 0.5),
        "gate_weight": normal_values(keys[5], (2, C, 2 * H), C ** -0.5, 0.5),
        "out_gain": jnp.clip(1.0 + 0.18 * jax.random.normal(keys[6], (2, H), jnp.float32), 0.1, 1.9),
        "out_bias": normal_values(keys[7], (2, H), 0.5, 3.0, (), jnp.float32),
        "final_weight": normal_values(keys[8], (2, H, C), H ** -0.5, 0.5),
        "output_gate": normal_values(keys[9], (2, C, C), C ** -0.5, 0.5),
    }


def normalize(values, gain_vector, bias_vector):
    average = lax.optimization_barrier(jnp.mean(values, axis=-1, keepdims=True))
    centred = values - average
    variance = lax.optimization_barrier(jnp.mean(centred * centred, axis=-1, keepdims=True))
    return centred * lax.rsqrt(variance + 1e-05) * gain_vector + bias_vector

def project(pair_map, pair_mask, norm_gain, norm_bias, proj_weight, gate_weight, output_gate, layer_id):
    normed = normalize(pair_map.astype(jnp.float32), norm_gain[layer_id], norm_bias[layer_id]).astype(jnp.bfloat16)
    projected = jnp.dot(normed, proj_weight[layer_id], preferred_element_type=jnp.float32)
    gating = jnp.dot(normed, gate_weight[layer_id], preferred_element_type=jnp.float32)
    halves = (jax.nn.sigmoid(gating) * projected * pair_mask[..., None]).astype(jnp.bfloat16)
    closing = jax.nn.sigmoid(jnp.dot(normed, output_gate[layer_id], preferred_element_type=jnp.float32))
    return (halves, closing)

def finish(pair_map, summed, closing, out_gain, out_bias, final_weight, layer_id):
    lifted = normalize(summed.astype(jnp.float32), out_gain[layer_id], out_bias[layer_id]).astype(jnp.bfloat16)
    update = closing * jnp.dot(lifted, final_weight[layer_id], preferred_element_type=jnp.float32)
    return (pair_map.astype(jnp.float32) + update).astype(jnp.bfloat16)

def reference(pair_map, token_mask, norm_gain, norm_bias, proj_weight, gate_weight, out_gain, out_bias, final_weight, output_gate):
    mask_float = token_mask.astype(jnp.float32)
    pair_mask = mask_float[:, None] * mask_float[None, :]
    halves, closing = project(pair_map, pair_mask, norm_gain, norm_bias, proj_weight, gate_weight, output_gate, 0)
    left_side = halves[..., :H].astype(jnp.float32)
    right_side = halves[..., H:].astype(jnp.float32)
    summed = jnp.einsum('ikh,jkh->ijh', left_side, right_side).astype(jnp.bfloat16)
    pair_map = finish(pair_map, summed, closing, out_gain, out_bias, final_weight, 0)
    halves, closing = project(pair_map, pair_mask, norm_gain, norm_bias, proj_weight, gate_weight, output_gate, 1)
    left_side = halves[..., :H].astype(jnp.float32)
    right_side = halves[..., H:].astype(jnp.float32)
    summed = jnp.einsum('kih,kjh->ijh', left_side, right_side).astype(jnp.bfloat16)
    return finish(pair_map, summed, closing, out_gain, out_bias, final_weight, 1)
```

```python
import functools

import jax
import jax.numpy as jnp
from jax import lax
from jax.experimental import pallas as pl
from jax.experimental.pallas import tpu as pltpu
from jax.sharding import PartitionSpec as P

LANES = 128
EPS = 1e-05
NT = (((1,), (1,)), ((), ()))
TN = (((0,), (0,)), ((), ()))


def double_sigmoid(half_x):
    return jnp.tanh(half_x) + 1.0


PER = 8
PAD = 1


def normalize_down(x, gain_col, bias_col):
    average = jnp.mean(x, axis=0, keepdims=True)
    centred = x - average
    variance = jnp.mean(centred * centred, axis=0, keepdims=True)
    return centred * lax.rsqrt(variance + EPS) * gain_col + bias_col


def column(row, width):
    return jnp.broadcast_to(row, (width, row.shape[1])).T


def group_at(slot, groups):
    return lax.rem(slot + groups - lax.rem(lax.axis_index("col"), groups), groups)


def load_down(z_ref, chunk, groups):
    lane_rows = z_ref.shape[0] // groups
    columns = [
        jnp.concatenate(
            [
                z_ref[chunk * PER + q + lane_rows * group_at(slot, groups)]
                for slot in range(groups)
            ],
            axis=0,
        ).astype(jnp.float32).T
        for q in range(PER)
    ]
    return jnp.concatenate(columns, axis=1)


def halves_weights(proj_ref, gate_ref, layer):
    half = jnp.asarray(0.5, jnp.bfloat16)
    return (proj_ref[layer] * half).T, (gate_ref[layer] * half).T


def project_chunk(chunk, normed, mask, weights, scratch):
    normed = (normed * mask).astype(jnp.bfloat16)
    projected = jnp.dot(weights[0], normed, preferred_element_type=jnp.float32)
    gating = jnp.dot(weights[1], normed, preferred_element_type=jnp.float32)
    halves = double_sigmoid(gating) * projected
    rows = halves.shape[0]
    for q in range(PER):
        first = (chunk * PER + q) * (rows + PAD)
        scratch[first : first + rows, :] = halves[:, q * LANES : (q + 1) * LANES]


def spread_halves(scratch, halves_ref, devices):
    count, slots, lane_rows, _ = halves_ref.shape
    per_device = slots // 2
    hidden = count * per_device
    for d in devices:
        for slot in range(slots):
            h = (slot // per_device) * hidden + d * per_device + slot % per_device
            rows = scratch[pl.ds(h, lane_rows, stride=2 * hidden + PAD), :]
            halves_ref[d, slot] = rows.astype(jnp.bfloat16)


def slots_kernel(cols, slots_ref):
    slots_ref[...] = lax.broadcasted_iota(jnp.int32, slots_ref.shape, 1) // cols


def first_kernel(
    groups, slots_ref, z_ref, gain_ref, bias_ref, proj_ref, gate_ref, mask_row_ref,
    halves_ref, mask_ref, mask_col_ref, scratch,
):
    rows, cols, _ = z_ref.shape
    tokens = mask_row_ref.shape[1]
    lane_rows = rows // groups

    shift = lax.rem(tokens - lax.axis_index("col") * cols, tokens)
    mask_row = mask_row_ref[...].astype(jnp.float32)
    from_here = pltpu.roll(jnp.broadcast_to(mask_row, (8, tokens)), shift, 1)[:, :LANES]
    col_mask = from_here
    for slot in range(1, groups):
        col_mask = jnp.where(
            slots_ref[...] == slot, pltpu.roll(from_here, slot * cols, 1), col_mask
        )
    mask_col_ref[...] = column(mask_row, LANES)
    first_row = lax.axis_index("row") * rows
    for s in range(lane_rows):
        row_mask = jnp.zeros((1, LANES), jnp.float32)
        for slot in range(groups):
            row = first_row + s + lane_rows * group_at(slot, groups)
            row_mask = jnp.where(
                slots_ref[0:1, :] == slot, mask_col_ref[pl.ds(row, 1), :], row_mask
            )
        lanes = slice((s % PER) * LANES, (s % PER + 1) * LANES)
        mask_ref[s // PER, :, lanes] = row_mask * col_mask[0:1]

    weights = halves_weights(proj_ref, gate_ref, 0)
    gain_col = column(gain_ref[0:1, :], PER * LANES)
    bias_col = column(bias_ref[0:1, :], PER * LANES)
    for chunk in range(lane_rows // PER):
        normed = normalize_down(load_down(z_ref, chunk, groups), gain_col, bias_col)
        project_chunk(chunk, normed, mask_ref[chunk], weights, scratch)
    spread_halves(scratch, halves_ref, range(halves_ref.shape[0]))


def gate_chunk(weight, normed):
    gating = jnp.dot(weight, normed.astype(jnp.bfloat16), preferred_element_type=jnp.float32)
    return double_sigmoid(gating)


def gate_weights(closer_ref, gain_ref, bias_ref, layer):
    weight = (closer_ref[layer] * jnp.asarray(0.5, jnp.bfloat16)).T
    gain_col = column(gain_ref[layer : layer + 1, :], PER * LANES)
    bias_col = column(bias_ref[layer : layer + 1, :], PER * LANES)
    return weight, gain_col, bias_col


def prepare_kernel(
    groups, z_ref, gain_ref, bias_ref, closer_ref, out_gain_ref, out_bias_ref, final_ref,
    proj_ref, gate_ref, mask_ref,
    z_down_ref, closing_ref, final_down_ref, weights_ref, rows_ref, mask_out_ref,
):
    mask_out_ref[...] = mask_ref[...]
    half = jnp.asarray(0.5, jnp.bfloat16)
    for layer in range(2):
        final_down_ref[layer] = (final_ref[layer] * half).T
    weights_ref[0], weights_ref[1] = halves_weights(proj_ref, gate_ref, 1)
    rows = [
        (out_gain_ref, 0), (out_bias_ref, 0), (gain_ref, 1), (bias_ref, 1), (out_gain_ref, 1),
        (out_bias_ref, 1),
    ]
    for n, (ref, layer) in enumerate(rows):
        rows_ref[n : n + 1, :] = ref[layer : layer + 1, :]
    weight, gain_col, bias_col = gate_weights(closer_ref, gain_ref, bias_ref, 0)

    def body(chunk, carry):
        z = load_down(z_ref, chunk, groups)
        z_down_ref[chunk] = z.astype(jnp.bfloat16)
        closing_ref[chunk] = gate_chunk(weight, normalize_down(z, gain_col, bias_col)).astype(
            jnp.bfloat16
        )
        return carry

    lax.fori_loop(0, z_down_ref.shape[0], body, 0, unroll=2)


def closing_kernel(z_down_ref, gain_ref, bias_ref, closer_ref, closing_ref):
    weight, gain_col, bias_col = gate_weights(closer_ref, gain_ref, bias_ref, 1)

    def body(chunk, carry):
        z = z_down_ref[chunk].astype(jnp.float32)
        closing_ref[chunk] = gate_chunk(weight, normalize_down(z, gain_col, bias_col)).astype(
            jnp.bfloat16
        )
        return carry

    lax.fori_loop(0, z_down_ref.shape[0], body, 0, unroll=2)


def finish_chunk(chunk, lane_rows, sums_scratch, gain_col, bias_col, final, closing_ref, z_down_ref):
    hidden = final.shape[1]
    summed = jnp.concatenate(
        [
            sums_scratch[pl.ds(chunk * PER + q, hidden, stride=lane_rows + PAD), :]
            for q in range(PER)
        ],
        axis=1,
    )
    lifted = normalize_down(summed, gain_col, bias_col).astype(jnp.bfloat16)
    update = jnp.dot(final, lifted, preferred_element_type=jnp.float32)
    return (z_down_ref[chunk].astype(jnp.float32) + closing_ref[chunk].astype(jnp.float32) * update).astype(
        jnp.bfloat16
    )


def load_sums(sums_ref, scratch):
    devices, per_device, lane_rows, _ = sums_ref.shape
    for d in range(devices):
        for slot in range(per_device):
            first = (d * per_device + slot) * (lane_rows + PAD)
            scratch[first : first + lane_rows, :] = sums_ref[d, slot].astype(jnp.float32)


def middle_kernel(
    z_down_ref, sums_ref, closing_ref, final_ref, weights_ref, rows_ref, mask_ref,
    halves_ref, z_out_ref, sums_scratch, scratch,
):
    lane_rows = sums_ref.shape[2]
    load_sums(sums_ref, sums_scratch)
    final = final_ref[0]
    weights = weights_ref[0], weights_ref[1]
    out_gain_col, out_bias_col, gain_col, bias_col = [
        column(rows_ref[n : n + 1, :], PER * LANES) for n in range(4)
    ]
    for chunk in range(lane_rows // PER):
        z = finish_chunk(
            chunk, lane_rows, sums_scratch, out_gain_col, out_bias_col, final, closing_ref,
            z_down_ref,
        )
        z_out_ref[chunk] = z
        normed = normalize_down(z.astype(jnp.float32), gain_col, bias_col)
        project_chunk(chunk, normed, mask_ref[chunk], weights, scratch)
    spread_halves(scratch, halves_ref, range(halves_ref.shape[0]))


def finish_kernel(
    groups, z_down_ref, sums_ref, closing_ref, final_ref, rows_ref, out_hbm, sums_scratch, out_ref, out_sems,
):
    lane_rows = sums_ref.shape[2]
    cols = LANES // groups
    load_sums(sums_ref, sums_scratch)
    final = final_ref[1]
    gain_col, bias_col = [column(rows_ref[n : n + 1, :], PER * LANES) for n in (4, 5)]
    copies = []
    for chunk in range(lane_rows // PER):
        z = finish_chunk(
            chunk, lane_rows, sums_scratch, gain_col, bias_col, final, closing_ref, z_down_ref
        ).astype(jnp.float32)
        parts = [
            z[:, q * LANES : (q + 1) * LANES].T.astype(jnp.bfloat16) for q in range(PER)
        ]
        for slot in range(groups):
            first = chunk * PER + lane_rows * group_at(slot, groups)
            for q in range(PER):
                out_ref[first + q] = parts[q][slot * cols : (slot + 1) * cols]
            some = pl.ds(first, PER)
            copy = pltpu.make_async_copy(
                out_ref.at[some], out_hbm.at[some], out_sems.at[chunk, slot]
            )
            copy.start()
            copies.append(copy)
    for copy in copies:
        copy.wait()


def triangle_kernel(layer, groups, mesh_rows, mesh_cols, halves_ref, sums_ref, left, right):
    per_device = sums_ref.shape[1]
    lane_rows = sums_ref.shape[2]
    cols = LANES // groups
    lane_slot = lax.broadcasted_iota(jnp.int32, (1, LANES), 1) // cols

    def pick(pieces):
        out = pieces[0]
        for n in range(1, groups):
            out = jnp.where(lane_slot == n, pieces[n], out)
        return out

    def turned(value, slots):
        places = slots * cols % LANES
        return pltpu.roll(value, places, 1) if places else value

    def assemble(slot, target):
        for r in range(mesh_rows):
            for t in range(mesh_cols // groups):
                blocks = [
                    halves_ref[r * mesh_cols + t * groups + u, slot] for u in range(groups)
                ]
                for g in range(groups):
                    piece = turned(pick([blocks[(n - g) % groups] for n in range(groups)]), -g)
                    first = (r * groups + g) * lane_rows
                    target[first : first + lane_rows, t * LANES : (t + 1) * LANES] = piece

    for q in range(per_device):
        assemble(q, left.at[q])
        assemble(per_device + q, right.at[q])
        summed = lax.dot_general(
            left[q], right[q], NT if layer == 0 else TN, preferred_element_type=jnp.float32
        ).astype(jnp.bfloat16)
        for r in range(mesh_rows):
            for t in range(mesh_cols // groups):
                blocks = [
                    turned(
                        summed[
                            (r * groups + g) * lane_rows : (r * groups + g + 1) * lane_rows,
                            t * LANES : (t + 1) * LANES,
                        ],
                        g,
                    )
                    for g in range(groups)
                ]
                for u in range(groups):
                    piece = pick([blocks[(n - u) % groups] for n in range(groups)])
                    sums_ref[r * mesh_cols + t * groups + u, q] = piece


def vmem(count):
    return [pl.BlockSpec(memory_space=pltpu.VMEM)] * count


def by_channel(mesh_rows, mesh_cols, pair_map, token_mask, norm_gain, norm_bias, proj_weight,
               gate_weight, out_gain, out_bias, final_weight, output_gate):
    rows, cols, channels = pair_map.shape
    hidden = proj_weight.shape[2] // 2
    tokens = token_mask.shape[0]
    devices = mesh_rows * mesh_cols
    per_device = hidden // devices
    groups = LANES // cols
    lane_rows = rows // groups
    chunks = lane_rows // PER
    params = pltpu.CompilerParams(vmem_limit_bytes=40 * 1024 * 1024)
    halves_type = jax.ShapeDtypeStruct((devices, 2 * per_device, lane_rows, LANES), jnp.bfloat16)
    sums_type = jax.ShapeDtypeStruct((devices, per_device, lane_rows, LANES), jnp.bfloat16)
    down_type = jax.ShapeDtypeStruct((chunks, channels, PER * LANES), jnp.bfloat16)
    closing_type = down_type
    mask_type = jax.ShapeDtypeStruct((chunks, 1, PER * LANES), jnp.float32)
    halves_scratch = pltpu.VMEM((lane_rows * (2 * hidden + PAD), LANES), jnp.float32)
    sums_scratch = pltpu.VMEM((hidden * (lane_rows + PAD), LANES), jnp.float32)
    hbm = pl.BlockSpec(memory_space=pltpu.HBM)
    closing_cost = pl.CostEstimate(
        flops=2 * rows * cols * channels * channels,
        bytes_accessed=8 * rows * cols * channels,
        transcendentals=rows * cols * channels,
    )

    def exchange(value):
        return lax.all_to_all(value, ("row", "col"), split_axis=0, concat_axis=0, tiled=True)

    def triangle(layer, halves):
        return pl.pallas_call(
            functools.partial(triangle_kernel, layer, groups, mesh_rows, mesh_cols),
            out_shape=sums_type,
            in_specs=vmem(1),
            out_specs=pl.BlockSpec(memory_space=pltpu.VMEM),
            scratch_shapes=[pltpu.VMEM((per_device, tokens, tokens), jnp.bfloat16)] * 2,
            compiler_params=params,
        )(halves)

    slots = pl.pallas_call(
        functools.partial(slots_kernel, cols),
        out_shape=jax.ShapeDtypeStruct((8, LANES), jnp.int32),
        out_specs=pl.BlockSpec(memory_space=pltpu.VMEM),
        compiler_params=params,
        cost_estimate=pl.CostEstimate(
            flops=10**9, bytes_accessed=8 * LANES * 4, transcendentals=0
        ),
    )()
    halves, mask = pl.pallas_call(
        functools.partial(first_kernel, groups),
        out_shape=(halves_type, mask_type),
        in_specs=vmem(7),
        out_specs=tuple(vmem(2)),
        scratch_shapes=[pltpu.VMEM((tokens, LANES), jnp.float32), halves_scratch],
        compiler_params=params,
    )(slots, pair_map, norm_gain, norm_bias, proj_weight, gate_weight,
      token_mask.reshape(1, tokens))
    arrived = exchange(halves)
    z_down, closing, final_down, weights, table, mask = pl.pallas_call(
        functools.partial(prepare_kernel, groups),
        out_shape=(
            down_type,
            closing_type,
            jax.ShapeDtypeStruct((2, channels, hidden), jnp.bfloat16),
            jax.ShapeDtypeStruct((2, 2 * hidden, channels), jnp.bfloat16),
            jax.ShapeDtypeStruct((8, channels), jnp.float32),
            mask_type,
        ),
        in_specs=vmem(10),
        out_specs=tuple(vmem(6)),
        compiler_params=params,
        cost_estimate=closing_cost,
    )(pair_map, norm_gain, norm_bias, output_gate, out_gain, out_bias, final_weight, proj_weight,
      gate_weight, mask)
    sums = exchange(triangle(0, arrived))
    halves, z_down = pl.pallas_call(
        middle_kernel,
        out_shape=(halves_type, down_type),
        in_specs=vmem(7),
        out_specs=tuple(vmem(2)),
        scratch_shapes=[sums_scratch, halves_scratch],
        compiler_params=params,
    )(z_down, sums, closing, final_down, weights, table, mask)
    arrived = exchange(halves)
    closing = pl.pallas_call(
        closing_kernel,
        out_shape=closing_type,
        in_specs=vmem(4),
        out_specs=pl.BlockSpec(memory_space=pltpu.VMEM),
        compiler_params=params,
        cost_estimate=closing_cost,
    )(z_down, norm_gain, norm_bias, output_gate)
    sums = exchange(triangle(1, arrived))
    return pl.pallas_call(
        functools.partial(finish_kernel, groups),
        out_shape=jax.ShapeDtypeStruct(pair_map.shape, jnp.bfloat16),
        in_specs=vmem(5),
        out_specs=hbm,
        scratch_shapes=[
            sums_scratch,
            pltpu.VMEM(pair_map.shape, jnp.bfloat16),
            pltpu.SemaphoreType.DMA((chunks, groups)),
        ],
        compiler_params=params,
    )(z_down, sums, closing, final_down, table)


def normalize(values, gain_vector, bias_vector):
    average = jnp.mean(values, axis=-1, keepdims=True)
    centred = values - average
    variance = jnp.mean(centred * centred, axis=-1, keepdims=True)
    return centred * lax.rsqrt(variance + EPS) * gain_vector + bias_vector


def project(
    pair_map, pair_mask, norm_gain, norm_bias, proj_weight, gate_weight, output_gate, layer_id
):
    normed = normalize(
        pair_map.astype(jnp.float32), norm_gain[layer_id], norm_bias[layer_id]
    ).astype(jnp.bfloat16)
    projected = jnp.dot(normed, proj_weight[layer_id], preferred_element_type=jnp.float32)
    gating = jnp.dot(normed, gate_weight[layer_id], preferred_element_type=jnp.float32)
    halves = (jax.nn.sigmoid(gating) * projected * pair_mask[..., None]).astype(jnp.bfloat16)
    closing = jax.nn.sigmoid(
        jnp.dot(normed, output_gate[layer_id], preferred_element_type=jnp.float32)
    )
    return (halves, closing)


def finish(pair_map, summed, closing, out_gain, out_bias, final_weight, layer_id):
    lifted = normalize(summed.astype(jnp.float32), out_gain[layer_id], out_bias[layer_id]).astype(
        jnp.bfloat16
    )
    update = closing * jnp.dot(lifted, final_weight[layer_id], preferred_element_type=jnp.float32)
    return (pair_map.astype(jnp.float32) + update).astype(jnp.bfloat16)


def by_block(pair_map, token_mask, norm_gain, norm_bias, proj_weight, gate_weight, out_gain,
             out_bias, final_weight, output_gate):
    rows_here = pair_map.shape[0]
    cols_here = pair_map.shape[1]
    hidden = proj_weight.shape[2] // 2
    row_mask = lax.dynamic_slice_in_dim(
        token_mask, lax.axis_index("row") * rows_here, rows_here
    ).astype(jnp.float32)
    col_mask = lax.dynamic_slice_in_dim(
        token_mask, lax.axis_index("col") * cols_here, cols_here
    ).astype(jnp.float32)
    pair_mask = row_mask[:, None] * col_mask[None, :]
    halves, closing = project(
        pair_map, pair_mask, norm_gain, norm_bias, proj_weight, gate_weight, output_gate, 0
    )
    left_side = halves[..., :hidden]
    right_side = halves[..., hidden:]
    right_rows = lax.all_gather(right_side, "row", axis=0, tiled=True)
    partial_value = jnp.einsum(
        "ikh,jkh->ijh", left_side, right_rows, preferred_element_type=jnp.float32
    )
    summed = lax.psum_scatter(partial_value, "col", scatter_dimension=1, tiled=True).astype(
        jnp.bfloat16
    )
    pair_map = finish(pair_map, summed, closing, out_gain, out_bias, final_weight, 0)
    halves, closing = project(
        pair_map, pair_mask, norm_gain, norm_bias, proj_weight, gate_weight, output_gate, 1
    )
    left_side = halves[..., :hidden]
    right_side = halves[..., hidden:]
    left_cols = lax.all_gather(left_side, "col", axis=1, tiled=True)
    partial_value = jnp.einsum(
        "kih,kjh->ijh", left_cols, right_side, preferred_element_type=jnp.float32
    )
    summed = lax.psum_scatter(partial_value, "row", scatter_dimension=0, tiled=True).astype(
        jnp.bfloat16
    )
    return finish(pair_map, summed, closing, out_gain, out_bias, final_weight, 1)


def solution(mesh):
    mesh_rows, mesh_cols = mesh.shape["row"], mesh.shape["col"]

    def shards(pair_map, token_mask, norm_gain, norm_bias, proj_weight, *rest):
        rows, cols, _ = pair_map.shape
        hidden = proj_weight.shape[2] // 2
        groups = max(LANES // cols, 1)
        fits = (
            hidden % (mesh_rows * mesh_cols) == 0
            and LANES % cols == 0
            and rows % (16 * groups) == 0
            and mesh_cols % groups == 0
        )
        args = (pair_map, token_mask, norm_gain, norm_bias, proj_weight, *rest)
        if fits:
            return by_channel(mesh_rows, mesh_cols, *args)
        return by_block(*args)

    return jax.shard_map(
        shards,
        mesh=mesh,
        in_specs=(P("row", "col", None), P(), P(), P(), P(), P(), P(), P(), P(), P()),
        out_specs=P("row", "col", None),
        check_vma=False,
    )
```

```python
import functools

import jax
import jax.numpy as jnp
from jax import lax
from jax.experimental import pallas as pl
from jax.experimental.pallas import tpu as pltpu
from jax.sharding import PartitionSpec as P

LANES = 128
EPS = 1e-05
NT = (((1,), (1,)), ((), ()))
TN = (((0,), (0,)), ((), ()))


def double_sigmoid(half_x):
    return jnp.tanh(half_x) + 1.0


PER = 16
PAD = 1


def normalize_down(x, gain_col, bias_col):
    average = jnp.mean(x, axis=0, keepdims=True)
    centred = x - average
    variance = jnp.mean(centred * centred, axis=0, keepdims=True)
    return centred * lax.rsqrt(variance + EPS) * gain_col + bias_col


def column(row, width):
    return jnp.broadcast_to(row, (width, row.shape[1])).T


def group_at(slot, groups):
    return lax.rem(slot + groups - lax.rem(lax.axis_index("col"), groups), groups)


def load_down(z_ref, chunk, groups):
    lane_rows = z_ref.shape[0] // groups
    columns = [
        jnp.concatenate(
            [
                z_ref[chunk * PER + q + lane_rows * group_at(slot, groups)]
                for slot in range(groups)
            ],
            axis=0,
        ).astype(jnp.float32).T
        for q in range(PER)
    ]
    return jnp.concatenate(columns, axis=1)


def halves_weights(proj_ref, gate_ref, layer):
    half = jnp.asarray(0.5, jnp.bfloat16)
    return (proj_ref[layer] * half).T, (gate_ref[layer] * half).T


def project_chunk(chunk, normed, mask, weights, scratch):
    normed = (normed * mask).astype(jnp.bfloat16)
    projected = jnp.dot(weights[0], normed, preferred_element_type=jnp.float32)
    gating = jnp.dot(weights[1], normed, preferred_element_type=jnp.float32)
    halves = double_sigmoid(gating) * projected
    rows = halves.shape[0]
    for q in range(PER):
        first = (chunk * PER + q) * (rows + PAD)
        scratch[first : first + rows, :] = halves[:, q * LANES : (q + 1) * LANES]


def spread_halves(scratch, halves_ref, devices):
    count, slots, lane_rows, _ = halves_ref.shape
    per_device = slots // 2
    hidden = count * per_device
    for d in devices:
        for slot in range(slots):
            h = (slot // per_device) * hidden + d * per_device + slot % per_device
            rows = scratch[pl.ds(h, lane_rows, stride=2 * hidden + PAD), :]
            halves_ref[d, slot] = rows.astype(jnp.bfloat16)


def slots_kernel(cols, slots_ref):
    slots_ref[...] = lax.broadcasted_iota(jnp.int32, slots_ref.shape, 1) // cols


def first_kernel(
    groups, slots_ref, z_ref, gain_ref, bias_ref, proj_ref, gate_ref, mask_row_ref, closer_ref,
    out_gain_ref, out_bias_ref, final_ref,
    halves_ref, mask_ref, z_down_ref, closing_ref, turned_ref, weights_ref, rows_ref,
    mask_col_ref, scratch,
):
    rows, cols, _ = z_ref.shape
    tokens = mask_row_ref.shape[1]
    lane_rows = rows // groups

    shift = lax.rem(tokens - lax.axis_index("col") * cols, tokens)
    mask_row = mask_row_ref[...].astype(jnp.float32)
    from_here = pltpu.roll(jnp.broadcast_to(mask_row, (8, tokens)), shift, 1)[:, :LANES]
    col_mask = from_here
    for slot in range(1, groups):
        col_mask = jnp.where(
            slots_ref[...] == slot, pltpu.roll(from_here, slot * cols, 1), col_mask
        )
    mask_col_ref[...] = column(mask_row, LANES)
    first_row = lax.axis_index("row") * rows
    for s in range(lane_rows):
        row_mask = jnp.zeros((1, LANES), jnp.float32)
        for slot in range(groups):
            row = first_row + s + lane_rows * group_at(slot, groups)
            row_mask = jnp.where(
                slots_ref[0:1, :] == slot, mask_col_ref[pl.ds(row, 1), :], row_mask
            )
        lanes = slice((s % PER) * LANES, (s % PER + 1) * LANES)
        mask_ref[s // PER, :, lanes] = row_mask * col_mask[0:1]

    half = jnp.asarray(0.5, jnp.bfloat16)
    turned_ref[0] = (final_ref[0] * half).T
    turned_ref[1] = (closer_ref[1] * half).T
    turned_ref[2] = (final_ref[1] * half).T
    weights_ref[0], weights_ref[1] = halves_weights(proj_ref, gate_ref, 1)
    table = [
        (out_gain_ref, 0), (out_bias_ref, 0), (gain_ref, 1), (bias_ref, 1), (out_gain_ref, 1),
        (out_bias_ref, 1),
    ]
    for n, (ref, layer) in enumerate(table):
        rows_ref[n : n + 1, :] = ref[layer : layer + 1, :]

    weights = halves_weights(proj_ref, gate_ref, 0)
    closer = (closer_ref[0] * half).T
    gain_col = column(gain_ref[0:1, :], PER * LANES)
    bias_col = column(bias_ref[0:1, :], PER * LANES)
    for chunk in range(lane_rows // PER):
        z = load_down(z_ref, chunk, groups)
        z_down_ref[chunk] = z.astype(jnp.bfloat16)
        normed = normalize_down(z, gain_col, bias_col)
        closing_ref[chunk] = gate_chunk(closer, normed)
        project_chunk(chunk, normed, mask_ref[chunk], weights, scratch)
    spread_halves(scratch, halves_ref, range(halves_ref.shape[0]))


def gate_chunk(weight, normed):
    gating = jnp.dot(weight, normed.astype(jnp.bfloat16), preferred_element_type=jnp.float32)
    return double_sigmoid(gating).astype(jnp.bfloat16)


def finish_chunk(chunk, lane_rows, sums_scratch, gain_col, bias_col, final, closing_ref, z_down_ref):
    hidden = final.shape[1]
    summed = jnp.concatenate(
        [
            sums_scratch[pl.ds(chunk * PER + q, hidden, stride=lane_rows + PAD), :]
            for q in range(PER)
        ],
        axis=1,
    )
    lifted = normalize_down(summed, gain_col, bias_col).astype(jnp.bfloat16)
    update = jnp.dot(final, lifted, preferred_element_type=jnp.float32)
    return (z_down_ref[chunk].astype(jnp.float32) + closing_ref[chunk].astype(jnp.float32) * update).astype(
        jnp.bfloat16
    )


def load_sums(sums_ref, scratch):
    devices, per_device, lane_rows, _ = sums_ref.shape
    for d in range(devices):
        for slot in range(per_device):
            first = (d * per_device + slot) * (lane_rows + PAD)
            scratch[first : first + lane_rows, :] = sums_ref[d, slot].astype(jnp.float32)


def middle_kernel(
    z_down_ref, sums_ref, closing_ref, turned_ref, weights_ref, rows_ref, mask_ref,
    halves_ref, z_out_ref, closing_out_ref, sums_scratch, scratch,
):
    lane_rows = sums_ref.shape[2]
    load_sums(sums_ref, sums_scratch)
    final, closer = turned_ref[0], turned_ref[1]
    weights = weights_ref[0], weights_ref[1]
    out_gain_col, out_bias_col, gain_col, bias_col = [
        column(rows_ref[n : n + 1, :], PER * LANES) for n in range(4)
    ]
    for chunk in range(lane_rows // PER):
        z = finish_chunk(
            chunk, lane_rows, sums_scratch, out_gain_col, out_bias_col, final, closing_ref,
            z_down_ref,
        )
        z_out_ref[chunk] = z
        normed = normalize_down(z.astype(jnp.float32), gain_col, bias_col)
        closing_out_ref[chunk] = gate_chunk(closer, normed)
        project_chunk(chunk, normed, mask_ref[chunk], weights, scratch)
    spread_halves(scratch, halves_ref, range(halves_ref.shape[0]))


def finish_kernel(
    groups, z_down_ref, sums_ref, closing_ref, turned_ref, rows_ref, out_hbm, sums_scratch, out_ref, out_sems,
):
    lane_rows = sums_ref.shape[2]
    cols = LANES // groups
    load_sums(sums_ref, sums_scratch)
    final = turned_ref[2]
    gain_col, bias_col = [column(rows_ref[n : n + 1, :], PER * LANES) for n in (4, 5)]
    copies = []
    for chunk in range(lane_rows // PER):
        z = finish_chunk(
            chunk, lane_rows, sums_scratch, gain_col, bias_col, final, closing_ref, z_down_ref
        ).astype(jnp.float32)
        half = PER // 2
        for first_q in range(0, PER, half):
            for q in range(first_q, first_q + half):
                part = z[:, q * LANES : (q + 1) * LANES].T.astype(jnp.bfloat16)
                for slot in range(groups):
                    row = chunk * PER + q + lane_rows * group_at(slot, groups)
                    out_ref[row] = part[slot * cols : (slot + 1) * cols]
            for slot in range(groups):
                row = chunk * PER + first_q + lane_rows * group_at(slot, groups)
                some = pl.ds(row, half)
                copy = pltpu.make_async_copy(
                    out_ref.at[some], out_hbm.at[some], out_sems.at[len(copies)]
                )
                copy.start()
                copies.append(copy)
    for copy in copies:
        copy.wait()


def triangle_kernel(
    layer, groups, mesh_rows, mesh_cols, halves_ref, sums_ref, left, right
):
    per_device = sums_ref.shape[1]
    lane_rows = sums_ref.shape[2]
    cols = LANES // groups
    lane_slot = lax.broadcasted_iota(jnp.int32, (1, LANES), 1) // cols

    def pick(pieces):
        out = pieces[0]
        for n in range(1, groups):
            out = jnp.where(lane_slot == n, pieces[n], out)
        return out

    def turned(value, slots):
        places = slots * cols % LANES
        return pltpu.roll(value, places, 1) if places else value

    def assemble(slot, target):
        for r in range(mesh_rows):
            for t in range(mesh_cols // groups):
                blocks = [
                    halves_ref[r * mesh_cols + t * groups + u, slot] for u in range(groups)
                ]
                for g in range(groups):
                    piece = turned(pick([blocks[(n - g) % groups] for n in range(groups)]), -g)
                    first = (r * groups + g) * lane_rows
                    target[first : first + lane_rows, t * LANES : (t + 1) * LANES] = piece

    for q in range(per_device):
        assemble(q, left.at[q])
        assemble(per_device + q, right.at[q])
        summed = lax.dot_general(
            left[q], right[q], NT if layer == 0 else TN, preferred_element_type=jnp.float32
        ).astype(jnp.bfloat16)
        for r in range(mesh_rows):
            for t in range(mesh_cols // groups):
                blocks = [
                    turned(
                        summed[
                            (r * groups + g) * lane_rows : (r * groups + g + 1) * lane_rows,
                            t * LANES : (t + 1) * LANES,
                        ],
                        g,
                    )
                    for g in range(groups)
                ]
                for u in range(groups):
                    piece = pick([blocks[(n - u) % groups] for n in range(groups)])
                    sums_ref[r * mesh_cols + t * groups + u, q] = piece


def vmem(count):
    return [pl.BlockSpec(memory_space=pltpu.VMEM)] * count


def by_channel(mesh_rows, mesh_cols, pair_map, token_mask, norm_gain, norm_bias, proj_weight,
               gate_weight, out_gain, out_bias, final_weight, output_gate):
    rows, cols, channels = pair_map.shape
    hidden = proj_weight.shape[2] // 2
    tokens = token_mask.shape[0]
    devices = mesh_rows * mesh_cols
    per_device = hidden // devices
    groups = LANES // cols
    lane_rows = rows // groups
    chunks = lane_rows // PER
    params = pltpu.CompilerParams(vmem_limit_bytes=40 * 1024 * 1024)
    halves_type = jax.ShapeDtypeStruct((devices, 2 * per_device, lane_rows, LANES), jnp.bfloat16)
    sums_type = jax.ShapeDtypeStruct((devices, per_device, lane_rows, LANES), jnp.bfloat16)
    down_type = jax.ShapeDtypeStruct((chunks, channels, PER * LANES), jnp.bfloat16)
    mask_type = jax.ShapeDtypeStruct((chunks, 1, PER * LANES), jnp.float32)
    halves_scratch = pltpu.VMEM(((lane_rows + 1) * (2 * hidden + PAD), LANES), jnp.float32)
    sums_scratch = pltpu.VMEM(((hidden + 1) * (lane_rows + PAD), LANES), jnp.float32)
    hbm = pl.BlockSpec(memory_space=pltpu.HBM)
    def exchange(value):
        return lax.all_to_all(value, ("row", "col"), split_axis=0, concat_axis=0, tiled=True)

    def triangle(layer, halves):
        return pl.pallas_call(
            functools.partial(triangle_kernel, layer, groups, mesh_rows, mesh_cols),
            out_shape=sums_type,
            in_specs=vmem(1),
            out_specs=pl.BlockSpec(memory_space=pltpu.VMEM),
            scratch_shapes=[pltpu.VMEM((per_device, tokens, tokens), jnp.bfloat16)] * 2,
            compiler_params=params,
        )(halves)

    slots = pl.pallas_call(
        functools.partial(slots_kernel, cols),
        out_shape=jax.ShapeDtypeStruct((8, LANES), jnp.int32),
        out_specs=pl.BlockSpec(memory_space=pltpu.VMEM),
        compiler_params=params,
        cost_estimate=pl.CostEstimate(
            flops=10**9, bytes_accessed=8 * LANES * 4, transcendentals=0
        ),
    )()
    halves, mask, z_down, closing, turned, weights, table = pl.pallas_call(
        functools.partial(first_kernel, groups),
        out_shape=(
            halves_type,
            mask_type,
            down_type,
            down_type,
            jax.ShapeDtypeStruct((3, channels, hidden), jnp.bfloat16),
            jax.ShapeDtypeStruct((2, 2 * hidden, channels), jnp.bfloat16),
            jax.ShapeDtypeStruct((8, channels), jnp.float32),
        ),
        in_specs=vmem(11),
        out_specs=tuple(vmem(7)),
        scratch_shapes=[pltpu.VMEM((tokens, LANES), jnp.float32), halves_scratch],
        compiler_params=params,
    )(slots, pair_map, norm_gain, norm_bias, proj_weight, gate_weight,
      token_mask.reshape(1, tokens), output_gate, out_gain, out_bias, final_weight)
    sums = exchange(triangle(0, exchange(halves)))
    halves, z_down, closing = pl.pallas_call(
        middle_kernel,
        out_shape=(halves_type, down_type, down_type),
        in_specs=vmem(7),
        out_specs=tuple(vmem(3)),
        scratch_shapes=[sums_scratch, halves_scratch],
        compiler_params=params,
    )(z_down, sums, closing, turned, weights, table, mask)
    sums = exchange(triangle(1, exchange(halves)))
    return pl.pallas_call(
        functools.partial(finish_kernel, groups),
        out_shape=jax.ShapeDtypeStruct(pair_map.shape, jnp.bfloat16),
        in_specs=vmem(5),
        out_specs=hbm,
        scratch_shapes=[
            sums_scratch,
            pltpu.VMEM(pair_map.shape, jnp.bfloat16),
            pltpu.SemaphoreType.DMA((2 * chunks * groups,)),
        ],
        compiler_params=params,
    )(z_down, sums, closing, turned, table)


def normalize(values, gain_vector, bias_vector):
    average = jnp.mean(values, axis=-1, keepdims=True)
    centred = values - average
    variance = jnp.mean(centred * centred, axis=-1, keepdims=True)
    return centred * lax.rsqrt(variance + EPS) * gain_vector + bias_vector


def project(
    pair_map, pair_mask, norm_gain, norm_bias, proj_weight, gate_weight, output_gate, layer_id
):
    normed = normalize(
        pair_map.astype(jnp.float32), norm_gain[layer_id], norm_bias[layer_id]
    ).astype(jnp.bfloat16)
    projected = jnp.dot(normed, proj_weight[layer_id], preferred_element_type=jnp.float32)
    gating = jnp.dot(normed, gate_weight[layer_id], preferred_element_type=jnp.float32)
    halves = (jax.nn.sigmoid(gating) * projected * pair_mask[..., None]).astype(jnp.bfloat16)
    closing = jax.nn.sigmoid(
        jnp.dot(normed, output_gate[layer_id], preferred_element_type=jnp.float32)
    )
    return (halves, closing)


def finish(pair_map, summed, closing, out_gain, out_bias, final_weight, layer_id):
    lifted = normalize(summed.astype(jnp.float32), out_gain[layer_id], out_bias[layer_id]).astype(
        jnp.bfloat16
    )
    update = closing * jnp.dot(lifted, final_weight[layer_id], preferred_element_type=jnp.float32)
    return (pair_map.astype(jnp.float32) + update).astype(jnp.bfloat16)


def by_block(pair_map, token_mask, norm_gain, norm_bias, proj_weight, gate_weight, out_gain,
             out_bias, final_weight, output_gate):
    rows_here = pair_map.shape[0]
    cols_here = pair_map.shape[1]
    hidden = proj_weight.shape[2] // 2
    row_mask = lax.dynamic_slice_in_dim(
        token_mask, lax.axis_index("row") * rows_here, rows_here
    ).astype(jnp.float32)
    col_mask = lax.dynamic_slice_in_dim(
        token_mask, lax.axis_index("col") * cols_here, cols_here
    ).astype(jnp.float32)
    pair_mask = row_mask[:, None] * col_mask[None, :]
    halves, closing = project(
        pair_map, pair_mask, norm_gain, norm_bias, proj_weight, gate_weight, output_gate, 0
    )
    left_side = halves[..., :hidden]
    right_side = halves[..., hidden:]
    right_rows = lax.all_gather(right_side, "row", axis=0, tiled=True)
    partial_value = jnp.einsum(
        "ikh,jkh->ijh", left_side, right_rows, preferred_element_type=jnp.float32
    )
    summed = lax.psum_scatter(partial_value, "col", scatter_dimension=1, tiled=True).astype(
        jnp.bfloat16
    )
    pair_map = finish(pair_map, summed, closing, out_gain, out_bias, final_weight, 0)
    halves, closing = project(
        pair_map, pair_mask, norm_gain, norm_bias, proj_weight, gate_weight, output_gate, 1
    )
    left_side = halves[..., :hidden]
    right_side = halves[..., hidden:]
    left_cols = lax.all_gather(left_side, "col", axis=1, tiled=True)
    partial_value = jnp.einsum(
        "kih,kjh->ijh", left_cols, right_side, preferred_element_type=jnp.float32
    )
    summed = lax.psum_scatter(partial_value, "row", scatter_dimension=0, tiled=True).astype(
        jnp.bfloat16
    )
    return finish(pair_map, summed, closing, out_gain, out_bias, final_weight, 1)


def solution(mesh):
    mesh_rows, mesh_cols = mesh.shape["row"], mesh.shape["col"]

    def shards(pair_map, token_mask, norm_gain, norm_bias, proj_weight, *rest):
        rows, cols, _ = pair_map.shape
        hidden = proj_weight.shape[2] // 2
        groups = max(LANES // cols, 1)
        fits = (
            hidden % (mesh_rows * mesh_cols) == 0
            and LANES % cols == 0
            and rows % (16 * groups) == 0
            and mesh_cols % groups == 0
        )
        args = (pair_map, token_mask, norm_gain, norm_bias, proj_weight, *rest)
        if fits:
            return by_channel(mesh_rows, mesh_cols, *args)
        return by_block(*args)

    return jax.shard_map(
        shards,
        mesh=mesh,
        in_specs=(P("row", "col", None), P(), P(), P(), P(), P(), P(), P(), P(), P()),
        out_specs=P("row", "col", None),
        check_vma=False,
    )
```

```python
import functools

import jax
import jax.numpy as jnp
from jax import lax
from jax.experimental import pallas as pl
from jax.experimental.pallas import tpu as pltpu
from jax.sharding import PartitionSpec as P

LANES = 128
EPS = 1e-05
NT = (((1,), (1,)), ((), ()))
TN = (((0,), (0,)), ((), ()))


def double_sigmoid(half_x):
    return jnp.tanh(half_x) + 1.0


PER = 8
PAD = 1


def normalize_down(x, gain_col, bias_col):
    average = jnp.mean(x, axis=0, keepdims=True)
    centred = x - average
    variance = jnp.mean(centred * centred, axis=0, keepdims=True)
    return centred * lax.rsqrt(variance + EPS) * gain_col + bias_col


def column(row, width):
    return jnp.broadcast_to(row, (width, row.shape[1])).T


def group_at(slot, groups):
    return lax.rem(slot + groups - lax.rem(lax.axis_index("col"), groups), groups)


def load_down(z_ref, chunk, groups):
    lane_rows = z_ref.shape[0] // groups
    columns = [
        jnp.concatenate(
            [
                z_ref[chunk * PER + q + lane_rows * group_at(slot, groups)]
                for slot in range(groups)
            ],
            axis=0,
        ).astype(jnp.float32).T
        for q in range(PER)
    ]
    return jnp.concatenate(columns, axis=1)


def stacked_weights(proj_ref, gate_ref, closer_ref, layer):
    half = jnp.asarray(0.5, jnp.bfloat16)
    return jnp.concatenate(
        [(ref[layer] * half).T for ref in (proj_ref, gate_ref, closer_ref)], axis=0
    )


def project_chunk(chunk, normed, mask, weights, scratch):
    product = jnp.dot(weights, normed.astype(jnp.bfloat16), preferred_element_type=jnp.float32)
    rows = (product.shape[0] - normed.shape[0]) // 2
    halves = double_sigmoid(product[rows : 2 * rows]) * (product[:rows] * mask)
    for q in range(PER):
        first = (chunk * PER + q) * (rows + PAD)
        scratch[first : first + rows, :] = halves[:, q * LANES : (q + 1) * LANES]
    return double_sigmoid(product[2 * rows :]).astype(jnp.bfloat16)


def spread_halves(scratch, halves_ref, devices):
    count, slots, lane_rows, _ = halves_ref.shape
    per_device = slots // 2
    hidden = count * per_device
    for d in devices:
        for slot in range(slots):
            h = (slot // per_device) * hidden + d * per_device + slot % per_device
            rows = scratch[pl.ds(h, lane_rows, stride=2 * hidden + PAD), :]
            halves_ref[d, slot] = rows.astype(jnp.bfloat16)


def slots_kernel(cols, slots_ref):
    slots_ref[...] = lax.broadcasted_iota(jnp.int32, slots_ref.shape, 1) // cols


def first_kernel(
    groups, slots_ref, z_ref, gain_ref, bias_ref, proj_ref, gate_ref, mask_row_ref, closer_ref,
    out_gain_ref, out_bias_ref, final_ref,
    halves_ref, mask_ref, z_down_ref, closing_ref, turned_ref, weights_ref, rows_ref,
    mask_col_ref, scratch,
):
    rows, cols, _ = z_ref.shape
    tokens = mask_row_ref.shape[1]
    lane_rows = rows // groups

    shift = lax.rem(tokens - lax.axis_index("col") * cols, tokens)
    mask_row = mask_row_ref[...].astype(jnp.float32)
    from_here = pltpu.roll(jnp.broadcast_to(mask_row, (8, tokens)), shift, 1)[:, :LANES]
    col_mask = from_here
    for slot in range(1, groups):
        col_mask = jnp.where(
            slots_ref[...] == slot, pltpu.roll(from_here, slot * cols, 1), col_mask
        )
    mask_col_ref[...] = column(mask_row, LANES)
    first_row = lax.axis_index("row") * rows
    for s in range(lane_rows):
        row_mask = jnp.zeros((1, LANES), jnp.float32)
        for slot in range(groups):
            row = first_row + s + lane_rows * group_at(slot, groups)
            row_mask = jnp.where(
                slots_ref[0:1, :] == slot, mask_col_ref[pl.ds(row, 1), :], row_mask
            )
        lanes = slice((s % PER) * LANES, (s % PER + 1) * LANES)
        mask_ref[s // PER, :, lanes] = row_mask * col_mask[0:1]

    half = jnp.asarray(0.5, jnp.bfloat16)
    turned_ref[0] = (final_ref[0] * half).T
    turned_ref[1] = (final_ref[1] * half).T
    weights_ref[...] = stacked_weights(proj_ref, gate_ref, closer_ref, 1)
    table = [
        (out_gain_ref, 0), (out_bias_ref, 0), (gain_ref, 1), (bias_ref, 1), (out_gain_ref, 1),
        (out_bias_ref, 1),
    ]
    for n, (ref, layer) in enumerate(table):
        rows_ref[n : n + 1, :] = ref[layer : layer + 1, :]

    weights = stacked_weights(proj_ref, gate_ref, closer_ref, 0)
    gain_col = column(gain_ref[0:1, :], PER * LANES)
    bias_col = column(bias_ref[0:1, :], PER * LANES)
    for chunk in range(lane_rows // PER):
        z = load_down(z_ref, chunk, groups)
        z_down_ref[chunk] = z.astype(jnp.bfloat16)
        normed = normalize_down(z, gain_col, bias_col)
        closing_ref[chunk] = project_chunk(chunk, normed, mask_ref[chunk], weights, scratch)
    spread_halves(scratch, halves_ref, range(halves_ref.shape[0]))


def finish_chunk(chunk, lane_rows, sums_scratch, gain_col, bias_col, final, closing_ref, z_down_ref):
    hidden = final.shape[1]
    summed = jnp.concatenate(
        [
            sums_scratch[pl.ds(chunk * PER + q, hidden, stride=lane_rows + PAD), :]
            for q in range(PER)
        ],
        axis=1,
    )
    lifted = normalize_down(summed, gain_col, bias_col).astype(jnp.bfloat16)
    update = jnp.dot(final, lifted, preferred_element_type=jnp.float32)
    return (z_down_ref[chunk].astype(jnp.float32) + closing_ref[chunk].astype(jnp.float32) * update).astype(
        jnp.bfloat16
    )


def load_sums(sums_ref, scratch):
    devices, per_device, lane_rows, _ = sums_ref.shape
    for d in range(devices):
        for slot in range(per_device):
            first = (d * per_device + slot) * (lane_rows + PAD)
            scratch[first : first + lane_rows, :] = sums_ref[d, slot].astype(jnp.float32)


def middle_kernel(
    z_down_ref, sums_ref, closing_ref, turned_ref, weights_ref, rows_ref, mask_ref,
    halves_ref, z_out_ref, closing_out_ref, sums_scratch, scratch,
):
    lane_rows = sums_ref.shape[2]
    load_sums(sums_ref, sums_scratch)
    final = turned_ref[0]
    weights = weights_ref[...]
    out_gain_col, out_bias_col, gain_col, bias_col = [
        column(rows_ref[n : n + 1, :], PER * LANES) for n in range(4)
    ]
    for chunk in range(lane_rows // PER):
        z = finish_chunk(
            chunk, lane_rows, sums_scratch, out_gain_col, out_bias_col, final, closing_ref,
            z_down_ref,
        )
        z_out_ref[chunk] = z
        normed = normalize_down(z.astype(jnp.float32), gain_col, bias_col)
        closing_out_ref[chunk] = project_chunk(chunk, normed, mask_ref[chunk], weights, scratch)
    spread_halves(scratch, halves_ref, range(halves_ref.shape[0]))


def finish_kernel(
    groups, z_down_ref, sums_ref, closing_ref, turned_ref, rows_ref, out_hbm, sums_scratch, out_ref, out_sems,
):
    lane_rows = sums_ref.shape[2]
    cols = LANES // groups
    load_sums(sums_ref, sums_scratch)
    final = turned_ref[1]
    gain_col, bias_col = [column(rows_ref[n : n + 1, :], PER * LANES) for n in (4, 5)]
    copies = []
    for chunk in range(lane_rows // PER):
        z = finish_chunk(
            chunk, lane_rows, sums_scratch, gain_col, bias_col, final, closing_ref, z_down_ref
        ).astype(jnp.float32)
        half = PER // 2
        for first_q in range(0, PER, half):
            for q in range(first_q, first_q + half):
                part = z[:, q * LANES : (q + 1) * LANES].T.astype(jnp.bfloat16)
                for slot in range(groups):
                    row = chunk * PER + q + lane_rows * group_at(slot, groups)
                    out_ref[row] = part[slot * cols : (slot + 1) * cols]
            for slot in range(groups):
                row = chunk * PER + first_q + lane_rows * group_at(slot, groups)
                some = pl.ds(row, half)
                copy = pltpu.make_async_copy(
                    out_ref.at[some], out_hbm.at[some], out_sems.at[len(copies)]
                )
                copy.start()
                copies.append(copy)
    for copy in copies:
        copy.wait()


def triangle_kernel(
    layer, groups, mesh_rows, mesh_cols, halves_ref, sums_ref, left, right
):
    per_device = sums_ref.shape[1]
    lane_rows = sums_ref.shape[2]
    cols = LANES // groups
    lane_slot = lax.broadcasted_iota(jnp.int32, (1, LANES), 1) // cols

    def pick(pieces):
        out = pieces[0]
        for n in range(1, groups):
            out = jnp.where(lane_slot == n, pieces[n], out)
        return out

    def turned(value, slots):
        places = slots * cols % LANES
        return pltpu.roll(value, places, 1) if places else value

    def assemble(slot, target):
        for r in range(mesh_rows):
            for t in range(mesh_cols // groups):
                blocks = [
                    halves_ref[r * mesh_cols + t * groups + u, slot] for u in range(groups)
                ]
                for g in range(groups):
                    piece = turned(pick([blocks[(n - g) % groups] for n in range(groups)]), -g)
                    first = (r * groups + g) * lane_rows
                    target[first : first + lane_rows, t * LANES : (t + 1) * LANES] = piece

    for q in range(per_device):
        assemble(q, left.at[q])
        assemble(per_device + q, right.at[q])
        summed = lax.dot_general(
            left[q], right[q], NT if layer == 0 else TN, preferred_element_type=jnp.float32
        ).astype(jnp.bfloat16)
        for r in range(mesh_rows):
            for t in range(mesh_cols // groups):
                blocks = [
                    turned(
                        summed[
                            (r * groups + g) * lane_rows : (r * groups + g + 1) * lane_rows,
                            t * LANES : (t + 1) * LANES,
                        ],
                        g,
                    )
                    for g in range(groups)
                ]
                for u in range(groups):
                    piece = pick([blocks[(n - u) % groups] for n in range(groups)])
                    sums_ref[r * mesh_cols + t * groups + u, q] = piece


def vmem(count):
    return [pl.BlockSpec(memory_space=pltpu.VMEM)] * count


def by_channel(mesh_rows, mesh_cols, pair_map, token_mask, norm_gain, norm_bias, proj_weight,
               gate_weight, out_gain, out_bias, final_weight, output_gate):
    rows, cols, channels = pair_map.shape
    hidden = proj_weight.shape[2] // 2
    tokens = token_mask.shape[0]
    devices = mesh_rows * mesh_cols
    per_device = hidden // devices
    groups = LANES // cols
    lane_rows = rows // groups
    chunks = lane_rows // PER
    params = pltpu.CompilerParams(vmem_limit_bytes=40 * 1024 * 1024)
    halves_type = jax.ShapeDtypeStruct((devices, 2 * per_device, lane_rows, LANES), jnp.bfloat16)
    sums_type = jax.ShapeDtypeStruct((devices, per_device, lane_rows, LANES), jnp.bfloat16)
    down_type = jax.ShapeDtypeStruct((chunks, channels, PER * LANES), jnp.bfloat16)
    mask_type = jax.ShapeDtypeStruct((chunks, 1, PER * LANES), jnp.float32)
    halves_scratch = pltpu.VMEM(((lane_rows + 1) * (2 * hidden + PAD), LANES), jnp.float32)
    sums_scratch = pltpu.VMEM(((hidden + 1) * (lane_rows + PAD), LANES), jnp.float32)
    hbm = pl.BlockSpec(memory_space=pltpu.HBM)
    def exchange(value):
        return lax.all_to_all(value, ("row", "col"), split_axis=0, concat_axis=0, tiled=True)

    def triangle(layer, halves):
        return pl.pallas_call(
            functools.partial(triangle_kernel, layer, groups, mesh_rows, mesh_cols),
            out_shape=sums_type,
            in_specs=vmem(1),
            out_specs=pl.BlockSpec(memory_space=pltpu.VMEM),
            scratch_shapes=[pltpu.VMEM((per_device, tokens, tokens), jnp.bfloat16)] * 2,
            compiler_params=params,
        )(halves)

    slots = pl.pallas_call(
        functools.partial(slots_kernel, cols),
        out_shape=jax.ShapeDtypeStruct((8, LANES), jnp.int32),
        out_specs=pl.BlockSpec(memory_space=pltpu.VMEM),
        compiler_params=params,
        cost_estimate=pl.CostEstimate(
            flops=10**9, bytes_accessed=8 * LANES * 4, transcendentals=0
        ),
    )()
    halves, mask, z_down, closing, turned, weights, table = pl.pallas_call(
        functools.partial(first_kernel, groups),
        out_shape=(
            halves_type,
            mask_type,
            down_type,
            down_type,
            jax.ShapeDtypeStruct((2, channels, hidden), jnp.bfloat16),
            jax.ShapeDtypeStruct((4 * hidden + channels, channels), jnp.bfloat16),
            jax.ShapeDtypeStruct((8, channels), jnp.float32),
        ),
        in_specs=vmem(11),
        out_specs=tuple(vmem(7)),
        scratch_shapes=[pltpu.VMEM((tokens, LANES), jnp.float32), halves_scratch],
        compiler_params=params,
    )(slots, pair_map, norm_gain, norm_bias, proj_weight, gate_weight,
      token_mask.reshape(1, tokens), output_gate, out_gain, out_bias, final_weight)
    sums = exchange(triangle(0, exchange(halves)))
    halves, z_down, closing = pl.pallas_call(
        middle_kernel,
        out_shape=(halves_type, down_type, down_type),
        in_specs=vmem(7),
        out_specs=tuple(vmem(3)),
        scratch_shapes=[sums_scratch, halves_scratch],
        compiler_params=params,
    )(z_down, sums, closing, turned, weights, table, mask)
    sums = exchange(triangle(1, exchange(halves)))
    return pl.pallas_call(
        functools.partial(finish_kernel, groups),
        out_shape=jax.ShapeDtypeStruct(pair_map.shape, jnp.bfloat16),
        in_specs=vmem(5),
        out_specs=hbm,
        scratch_shapes=[
            sums_scratch,
            pltpu.VMEM(pair_map.shape, jnp.bfloat16),
            pltpu.SemaphoreType.DMA((2 * chunks * groups,)),
        ],
        compiler_params=params,
    )(z_down, sums, closing, turned, table)


def normalize(values, gain_vector, bias_vector):
    average = jnp.mean(values, axis=-1, keepdims=True)
    centred = values - average
    variance = jnp.mean(centred * centred, axis=-1, keepdims=True)
    return centred * lax.rsqrt(variance + EPS) * gain_vector + bias_vector


def project(
    pair_map, pair_mask, norm_gain, norm_bias, proj_weight, gate_weight, output_gate, layer_id
):
    normed = normalize(
        pair_map.astype(jnp.float32), norm_gain[layer_id], norm_bias[layer_id]
    ).astype(jnp.bfloat16)
    projected = jnp.dot(normed, proj_weight[layer_id], preferred_element_type=jnp.float32)
    gating = jnp.dot(normed, gate_weight[layer_id], preferred_element_type=jnp.float32)
    halves = (jax.nn.sigmoid(gating) * projected * pair_mask[..., None]).astype(jnp.bfloat16)
    closing = jax.nn.sigmoid(
        jnp.dot(normed, output_gate[layer_id], preferred_element_type=jnp.float32)
    )
    return (halves, closing)


def finish(pair_map, summed, closing, out_gain, out_bias, final_weight, layer_id):
    lifted = normalize(summed.astype(jnp.float32), out_gain[layer_id], out_bias[layer_id]).astype(
        jnp.bfloat16
    )
    update = closing * jnp.dot(lifted, final_weight[layer_id], preferred_element_type=jnp.float32)
    return (pair_map.astype(jnp.float32) + update).astype(jnp.bfloat16)


def by_block(pair_map, token_mask, norm_gain, norm_bias, proj_weight, gate_weight, out_gain,
             out_bias, final_weight, output_gate):
    rows_here = pair_map.shape[0]
    cols_here = pair_map.shape[1]
    hidden = proj_weight.shape[2] // 2
    row_mask = lax.dynamic_slice_in_dim(
        token_mask, lax.axis_index("row") * rows_here, rows_here
    ).astype(jnp.float32)
    col_mask = lax.dynamic_slice_in_dim(
        token_mask, lax.axis_index("col") * cols_here, cols_here
    ).astype(jnp.float32)
    pair_mask = row_mask[:, None] * col_mask[None, :]
    halves, closing = project(
        pair_map, pair_mask, norm_gain, norm_bias, proj_weight, gate_weight, output_gate, 0
    )
    left_side = halves[..., :hidden]
    right_side = halves[..., hidden:]
    right_rows = lax.all_gather(right_side, "row", axis=0, tiled=True)
    partial_value = jnp.einsum(
        "ikh,jkh->ijh", left_side, right_rows, preferred_element_type=jnp.float32
    )
    summed = lax.psum_scatter(partial_value, "col", scatter_dimension=1, tiled=True).astype(
        jnp.bfloat16
    )
    pair_map = finish(pair_map, summed, closing, out_gain, out_bias, final_weight, 0)
    halves, closing = project(
        pair_map, pair_mask, norm_gain, norm_bias, proj_weight, gate_weight, output_gate, 1
    )
    left_side = halves[..., :hidden]
    right_side = halves[..., hidden:]
    left_cols = lax.all_gather(left_side, "col", axis=1, tiled=True)
    partial_value = jnp.einsum(
        "kih,kjh->ijh", left_cols, right_side, preferred_element_type=jnp.float32
    )
    summed = lax.psum_scatter(partial_value, "row", scatter_dimension=0, tiled=True).astype(
        jnp.bfloat16
    )
    return finish(pair_map, summed, closing, out_gain, out_bias, final_weight, 1)


def solution(mesh):
    mesh_rows, mesh_cols = mesh.shape["row"], mesh.shape["col"]

    def shards(pair_map, token_mask, norm_gain, norm_bias, proj_weight, *rest):
        rows, cols, _ = pair_map.shape
        hidden = proj_weight.shape[2] // 2
        groups = max(LANES // cols, 1)
        fits = (
            hidden % (mesh_rows * mesh_cols) == 0
            and LANES % cols == 0
            and rows % (16 * groups) == 0
            and mesh_cols % groups == 0
        )
        args = (pair_map, token_mask, norm_gain, norm_bias, proj_weight, *rest)
        if fits:
            return by_channel(mesh_rows, mesh_cols, *args)
        return by_block(*args)

    return jax.shard_map(
        shards,
        mesh=mesh,
        in_specs=(P("row", "col", None), P(), P(), P(), P(), P(), P(), P(), P(), P()),
        out_specs=P("row", "col", None),
        check_vma=False,
    )
```

```python
import functools

import jax
import jax.numpy as jnp
from jax import lax
from jax.experimental import pallas as pl
from jax.experimental.pallas import tpu as pltpu
from jax.sharding import PartitionSpec as P

LANES = 128
EPS = 1e-05
NT = (((1,), (1,)), ((), ()))
TN = (((0,), (0,)), ((), ()))


def double_sigmoid(half_x):
    return jnp.tanh(half_x) + 1.0


PER = 8
PAD = 1


def normalize_down(x, gain_col, bias_col):
    average = jnp.mean(x, axis=0, keepdims=True)
    centred = x - average
    variance = jnp.mean(centred * centred, axis=0, keepdims=True)
    return centred * lax.rsqrt(variance + EPS) * gain_col + bias_col


def column(row, width):
    turned = jnp.broadcast_to(row, (LANES, row.shape[1])).T
    return jnp.concatenate([turned] * (width // LANES), axis=1)


def group_at(slot, groups):
    return lax.rem(slot + groups - lax.rem(lax.axis_index("col"), groups), groups)


def load_down(z_ref, chunk, groups):
    lane_rows = z_ref.shape[0] // groups
    columns = [
        jnp.concatenate(
            [
                z_ref[chunk * PER + q + lane_rows * group_at(slot, groups)]
                for slot in range(groups)
            ],
            axis=0,
        ).astype(jnp.float32).T
        for q in range(PER)
    ]
    return jnp.concatenate(columns, axis=1)


def halves_weights(proj_ref, gate_ref, layer):
    half = jnp.asarray(0.5, jnp.bfloat16)
    return (proj_ref[layer] * half).T, (gate_ref[layer] * half).T


def project_chunk(chunk, normed, mask, weights, scratch):
    normed = (normed * mask).astype(jnp.bfloat16)
    projected = jnp.dot(weights[0], normed, preferred_element_type=jnp.float32)
    gating = jnp.dot(weights[1], normed, preferred_element_type=jnp.float32)
    halves = double_sigmoid(gating) * projected
    rows = halves.shape[0]
    for q in range(PER):
        first = (chunk * PER + q) * (rows + PAD)
        scratch[first : first + rows, :] = halves[:, q * LANES : (q + 1) * LANES]


def spread_halves(scratch, halves_ref, devices):
    count, slots, lane_rows, _ = halves_ref.shape
    per_device = slots // 2
    hidden = count * per_device
    for d in devices:
        for slot in range(slots):
            h = (slot // per_device) * hidden + d * per_device + slot % per_device
            rows = scratch[pl.ds(h, lane_rows, stride=2 * hidden + PAD), :]
            halves_ref[d, slot] = rows.astype(jnp.bfloat16)


def slots_kernel(cols, slots_ref):
    slots_ref[...] = lax.broadcasted_iota(jnp.int32, slots_ref.shape, 1) // cols


def first_kernel(
    groups, slots_ref, z_ref, gain_ref, bias_ref, proj_ref, gate_ref, mask_row_ref, closer_ref,
    out_gain_ref, out_bias_ref, final_ref,
    halves_ref, mask_ref, z_down_ref, closing_ref, turned_ref, weights_ref, rows_ref,
    mask_col_ref, scratch,
):
    rows, cols, _ = z_ref.shape
    tokens = mask_row_ref.shape[1]
    lane_rows = rows // groups

    shift = lax.rem(tokens - lax.axis_index("col") * cols, tokens)
    mask_row = mask_row_ref[...].astype(jnp.float32)
    from_here = pltpu.roll(jnp.broadcast_to(mask_row, (8, tokens)), shift, 1)[:, :LANES]
    col_mask = from_here
    for slot in range(1, groups):
        col_mask = jnp.where(
            slots_ref[...] == slot, pltpu.roll(from_here, slot * cols, 1), col_mask
        )
    mask_col_ref[...] = column(mask_row, LANES)
    first_row = lax.axis_index("row") * rows
    for s in range(lane_rows):
        row_mask = jnp.zeros((1, LANES), jnp.float32)
        for slot in range(groups):
            row = first_row + s + lane_rows * group_at(slot, groups)
            row_mask = jnp.where(
                slots_ref[0:1, :] == slot, mask_col_ref[pl.ds(row, 1), :], row_mask
            )
        lanes = slice((s % PER) * LANES, (s % PER + 1) * LANES)
        mask_ref[s // PER, :, lanes] = row_mask * col_mask[0:1]

    half = jnp.asarray(0.5, jnp.bfloat16)
    turned_ref[0] = (final_ref[0] * half).T
    turned_ref[1] = (closer_ref[1] * half).T
    turned_ref[2] = (final_ref[1] * half).T
    weights_ref[0], weights_ref[1] = halves_weights(proj_ref, gate_ref, 1)
    table = [
        (out_gain_ref, 0), (out_bias_ref, 0), (gain_ref, 1), (bias_ref, 1), (out_gain_ref, 1),
        (out_bias_ref, 1),
    ]
    for n, (ref, layer) in enumerate(table):
        rows_ref[n : n + 1, :] = ref[layer : layer + 1, :]

    weights = halves_weights(proj_ref, gate_ref, 0)
    closer = (closer_ref[0] * half).T
    gain_col = column(gain_ref[0:1, :], PER * LANES)
    bias_col = column(bias_ref[0:1, :], PER * LANES)
    for chunk in range(lane_rows // PER):
        z = load_down(z_ref, chunk, groups)
        z_down_ref[chunk] = z.astype(jnp.bfloat16)
        normed = normalize_down(z, gain_col, bias_col)
        closing_ref[chunk] = gate_chunk(closer, normed)
        project_chunk(chunk, normed, mask_ref[chunk], weights, scratch)
    spread_halves(scratch, halves_ref, range(halves_ref.shape[0]))


def gate_chunk(weight, normed):
    gating = jnp.dot(weight, normed.astype(jnp.bfloat16), preferred_element_type=jnp.float32)
    return double_sigmoid(gating).astype(jnp.bfloat16)


def finish_chunk(chunk, lane_rows, sums_scratch, gain_col, bias_col, final, closing_ref, z_down_ref):
    hidden = final.shape[1]
    summed = jnp.concatenate(
        [
            sums_scratch[pl.ds(chunk * PER + q, hidden, stride=lane_rows + PAD), :]
            for q in range(PER)
        ],
        axis=1,
    )
    lifted = normalize_down(summed, gain_col, bias_col).astype(jnp.bfloat16)
    update = jnp.dot(final, lifted, preferred_element_type=jnp.float32)
    return (z_down_ref[chunk].astype(jnp.float32) + closing_ref[chunk].astype(jnp.float32) * update).astype(
        jnp.bfloat16
    )


def load_sums(sums_ref, scratch):
    devices, per_device, lane_rows, _ = sums_ref.shape
    for d in range(devices):
        for slot in range(per_device):
            first = (d * per_device + slot) * (lane_rows + PAD)
            scratch[first : first + lane_rows, :] = sums_ref[d, slot].astype(jnp.float32)


def middle_kernel(
    z_down_ref, sums_ref, closing_ref, turned_ref, weights_ref, rows_ref, mask_ref,
    halves_ref, z_out_ref, closing_out_ref, sums_scratch, scratch,
):
    lane_rows = sums_ref.shape[2]
    load_sums(sums_ref, sums_scratch)
    final, closer = turned_ref[0], turned_ref[1]
    weights = weights_ref[0], weights_ref[1]
    out_gain_col, out_bias_col, gain_col, bias_col = [
        column(rows_ref[n : n + 1, :], PER * LANES) for n in range(4)
    ]
    for chunk in range(lane_rows // PER):
        z = finish_chunk(
            chunk, lane_rows, sums_scratch, out_gain_col, out_bias_col, final, closing_ref,
            z_down_ref,
        )
        z_out_ref[chunk] = z
        normed = normalize_down(z.astype(jnp.float32), gain_col, bias_col)
        closing_out_ref[chunk] = gate_chunk(closer, normed)
        project_chunk(chunk, normed, mask_ref[chunk], weights, scratch)
    spread_halves(scratch, halves_ref, range(halves_ref.shape[0]))


def finish_kernel(
    groups, z_down_ref, sums_ref, closing_ref, turned_ref, rows_ref, out_hbm, sums_scratch, out_ref, out_sems,
):
    lane_rows = sums_ref.shape[2]
    cols = LANES // groups
    load_sums(sums_ref, sums_scratch)
    final = turned_ref[2]
    gain_col, bias_col = [column(rows_ref[n : n + 1, :], PER * LANES) for n in (4, 5)]
    copies = []
    for chunk in range(lane_rows // PER):
        z = finish_chunk(
            chunk, lane_rows, sums_scratch, gain_col, bias_col, final, closing_ref, z_down_ref
        ).astype(jnp.float32)
        half = PER // 2
        for first_q in range(0, PER, half):
            for q in range(first_q, first_q + half):
                part = z[:, q * LANES : (q + 1) * LANES].T.astype(jnp.bfloat16)
                for slot in range(groups):
                    row = chunk * PER + q + lane_rows * group_at(slot, groups)
                    out_ref[row] = part[slot * cols : (slot + 1) * cols]
            for slot in range(groups):
                row = chunk * PER + first_q + lane_rows * group_at(slot, groups)
                some = pl.ds(row, half)
                copy = pltpu.make_async_copy(
                    out_ref.at[some], out_hbm.at[some], out_sems.at[len(copies)]
                )
                copy.start()
                copies.append(copy)
    for copy in copies:
        copy.wait()


def triangle_kernel(
    layer, groups, mesh_rows, mesh_cols, halves_ref, sums_ref, left, right
):
    per_device = sums_ref.shape[1]
    lane_rows = sums_ref.shape[2]
    cols = LANES // groups
    lane_slot = lax.broadcasted_iota(jnp.int32, (1, LANES), 1) // cols

    def pick(pieces):
        out = pieces[0]
        for n in range(1, groups):
            out = jnp.where(lane_slot == n, pieces[n], out)
        return out

    def turned(value, slots):
        places = slots * cols % LANES
        return pltpu.roll(value, places, 1) if places else value

    def assemble(slot, target):
        for r in range(mesh_rows):
            for t in range(mesh_cols // groups):
                blocks = [
                    halves_ref[r * mesh_cols + t * groups + u, slot] for u in range(groups)
                ]
                for g in range(groups):
                    piece = turned(pick([blocks[(n - g) % groups] for n in range(groups)]), -g)
                    first = (r * groups + g) * lane_rows
                    target[first : first + lane_rows, t * LANES : (t + 1) * LANES] = piece

    for q in range(per_device):
        assemble(q, left.at[q])
        assemble(per_device + q, right.at[q])
        summed = lax.dot_general(
            left[q], right[q], NT if layer == 0 else TN, preferred_element_type=jnp.float32
        ).astype(jnp.bfloat16)
        for r in range(mesh_rows):
            for t in range(mesh_cols // groups):
                blocks = [
                    turned(
                        summed[
                            (r * groups + g) * lane_rows : (r * groups + g + 1) * lane_rows,
                            t * LANES : (t + 1) * LANES,
                        ],
                        g,
                    )
                    for g in range(groups)
                ]
                for u in range(groups):
                    piece = pick([blocks[(n - u) % groups] for n in range(groups)])
                    sums_ref[r * mesh_cols + t * groups + u, q] = piece


def vmem(count):
    return [pl.BlockSpec(memory_space=pltpu.VMEM)] * count


def by_channel(mesh_rows, mesh_cols, pair_map, token_mask, norm_gain, norm_bias, proj_weight,
               gate_weight, out_gain, out_bias, final_weight, output_gate):
    rows, cols, channels = pair_map.shape
    hidden = proj_weight.shape[2] // 2
    tokens = token_mask.shape[0]
    devices = mesh_rows * mesh_cols
    per_device = hidden // devices
    groups = LANES // cols
    lane_rows = rows // groups
    chunks = lane_rows // PER
    params = pltpu.CompilerParams(vmem_limit_bytes=40 * 1024 * 1024)
    halves_type = jax.ShapeDtypeStruct((devices, 2 * per_device, lane_rows, LANES), jnp.bfloat16)
    sums_type = jax.ShapeDtypeStruct((devices, per_device, lane_rows, LANES), jnp.bfloat16)
    down_type = jax.ShapeDtypeStruct((chunks, channels, PER * LANES), jnp.bfloat16)
    mask_type = jax.ShapeDtypeStruct((chunks, 1, PER * LANES), jnp.float32)
    halves_scratch = pltpu.VMEM(((lane_rows + 1) * (2 * hidden + PAD), LANES), jnp.float32)
    sums_scratch = pltpu.VMEM(((hidden + 1) * (lane_rows + PAD), LANES), jnp.float32)
    hbm = pl.BlockSpec(memory_space=pltpu.HBM)
    def exchange(value):
        return lax.all_to_all(value, ("row", "col"), split_axis=0, concat_axis=0, tiled=True)

    def triangle(layer, halves):
        return pl.pallas_call(
            functools.partial(triangle_kernel, layer, groups, mesh_rows, mesh_cols),
            out_shape=sums_type,
            in_specs=vmem(1),
            out_specs=pl.BlockSpec(memory_space=pltpu.VMEM),
            scratch_shapes=[pltpu.VMEM((per_device, tokens, tokens), jnp.bfloat16)] * 2,
            compiler_params=params,
        )(halves)

    slots = pl.pallas_call(
        functools.partial(slots_kernel, cols),
        out_shape=jax.ShapeDtypeStruct((8, LANES), jnp.int32),
        out_specs=pl.BlockSpec(memory_space=pltpu.VMEM),
        compiler_params=params,
        cost_estimate=pl.CostEstimate(
            flops=10**9, bytes_accessed=8 * LANES * 4, transcendentals=0
        ),
    )()
    halves, mask, z_down, closing, turned, weights, table = pl.pallas_call(
        functools.partial(first_kernel, groups),
        out_shape=(
            halves_type,
            mask_type,
            down_type,
            down_type,
            jax.ShapeDtypeStruct((3, channels, hidden), jnp.bfloat16),
            jax.ShapeDtypeStruct((2, 2 * hidden, channels), jnp.bfloat16),
            jax.ShapeDtypeStruct((8, channels), jnp.float32),
        ),
        in_specs=vmem(11),
        out_specs=tuple(vmem(7)),
        scratch_shapes=[pltpu.VMEM((tokens, LANES), jnp.float32), halves_scratch],
        compiler_params=params,
    )(slots, pair_map, norm_gain, norm_bias, proj_weight, gate_weight,
      token_mask.reshape(1, tokens), output_gate, out_gain, out_bias, final_weight)
    sums = exchange(triangle(0, exchange(halves)))
    halves, z_down, closing = pl.pallas_call(
        middle_kernel,
        out_shape=(halves_type, down_type, down_type),
        in_specs=vmem(7),
        out_specs=tuple(vmem(3)),
        scratch_shapes=[sums_scratch, halves_scratch],
        compiler_params=params,
    )(z_down, sums, closing, turned, weights, table, mask)
    sums = exchange(triangle(1, exchange(halves)))
    return pl.pallas_call(
        functools.partial(finish_kernel, groups),
        out_shape=jax.ShapeDtypeStruct(pair_map.shape, jnp.bfloat16),
        in_specs=vmem(5),
        out_specs=hbm,
        scratch_shapes=[
            sums_scratch,
            pltpu.VMEM(pair_map.shape, jnp.bfloat16),
            pltpu.SemaphoreType.DMA((2 * chunks * groups,)),
        ],
        compiler_params=params,
    )(z_down, sums, closing, turned, table)


def normalize(values, gain_vector, bias_vector):
    average = jnp.mean(values, axis=-1, keepdims=True)
    centred = values - average
    variance = jnp.mean(centred * centred, axis=-1, keepdims=True)
    return centred * lax.rsqrt(variance + EPS) * gain_vector + bias_vector


def project(
    pair_map, pair_mask, norm_gain, norm_bias, proj_weight, gate_weight, output_gate, layer_id
):
    normed = normalize(
        pair_map.astype(jnp.float32), norm_gain[layer_id], norm_bias[layer_id]
    ).astype(jnp.bfloat16)
    projected = jnp.dot(normed, proj_weight[layer_id], preferred_element_type=jnp.float32)
    gating = jnp.dot(normed, gate_weight[layer_id], preferred_element_type=jnp.float32)
    halves = (jax.nn.sigmoid(gating) * projected * pair_mask[..., None]).astype(jnp.bfloat16)
    closing = jax.nn.sigmoid(
        jnp.dot(normed, output_gate[layer_id], preferred_element_type=jnp.float32)
    )
    return (halves, closing)


def finish(pair_map, summed, closing, out_gain, out_bias, final_weight, layer_id):
    lifted = normalize(summed.astype(jnp.float32), out_gain[layer_id], out_bias[layer_id]).astype(
        jnp.bfloat16
    )
    update = closing * jnp.dot(lifted, final_weight[layer_id], preferred_element_type=jnp.float32)
    return (pair_map.astype(jnp.float32) + update).astype(jnp.bfloat16)


def by_block(pair_map, token_mask, norm_gain, norm_bias, proj_weight, gate_weight, out_gain,
             out_bias, final_weight, output_gate):
    rows_here = pair_map.shape[0]
    cols_here = pair_map.shape[1]
    hidden = proj_weight.shape[2] // 2
    row_mask = lax.dynamic_slice_in_dim(
        token_mask, lax.axis_index("row") * rows_here, rows_here
    ).astype(jnp.float32)
    col_mask = lax.dynamic_slice_in_dim(
        token_mask, lax.axis_index("col") * cols_here, cols_here
    ).astype(jnp.float32)
    pair_mask = row_mask[:, None] * col_mask[None, :]
    halves, closing = project(
        pair_map, pair_mask, norm_gain, norm_bias, proj_weight, gate_weight, output_gate, 0
    )
    left_side = halves[..., :hidden]
    right_side = halves[..., hidden:]
    right_rows = lax.all_gather(right_side, "row", axis=0, tiled=True)
    partial_value = jnp.einsum(
        "ikh,jkh->ijh", left_side, right_rows, preferred_element_type=jnp.float32
    )
    summed = lax.psum_scatter(partial_value, "col", scatter_dimension=1, tiled=True).astype(
        jnp.bfloat16
    )
    pair_map = finish(pair_map, summed, closing, out_gain, out_bias, final_weight, 0)
    halves, closing = project(
        pair_map, pair_mask, norm_gain, norm_bias, proj_weight, gate_weight, output_gate, 1
    )
    left_side = halves[..., :hidden]
    right_side = halves[..., hidden:]
    left_cols = lax.all_gather(left_side, "col", axis=1, tiled=True)
    partial_value = jnp.einsum(
        "kih,kjh->ijh", left_cols, right_side, preferred_element_type=jnp.float32
    )
    summed = lax.psum_scatter(partial_value, "row", scatter_dimension=0, tiled=True).astype(
        jnp.bfloat16
    )
    return finish(pair_map, summed, closing, out_gain, out_bias, final_weight, 1)


def solution(mesh):
    mesh_rows, mesh_cols = mesh.shape["row"], mesh.shape["col"]

    def shards(pair_map, token_mask, norm_gain, norm_bias, proj_weight, *rest):
        rows, cols, _ = pair_map.shape
        hidden = proj_weight.shape[2] // 2
        groups = max(LANES // cols, 1)
        fits = (
            hidden % (mesh_rows * mesh_cols) == 0
            and LANES % cols == 0
            and rows % (16 * groups) == 0
            and mesh_cols % groups == 0
        )
        args = (pair_map, token_mask, norm_gain, norm_bias, proj_weight, *rest)
        if fits:
            return by_channel(mesh_rows, mesh_cols, *args)
        return by_block(*args)

    return jax.shard_map(
        shards,
        mesh=mesh,
        in_specs=(P("row", "col", None), P(), P(), P(), P(), P(), P(), P(), P(), P()),
        out_specs=P("row", "col", None),
        check_vma=False,
    )
```

```python
import functools

import jax
import jax.numpy as jnp
from jax import lax
from jax.experimental import pallas as pl
from jax.experimental.pallas import tpu as pltpu
from jax.sharding import PartitionSpec as P

LANES = 128
EPS = 1e-05
NT = (((1,), (1,)), ((), ()))
TN = (((0,), (0,)), ((), ()))


def double_sigmoid(half_x):
    return jnp.tanh(half_x) + 1.0


PER = 8
PAD = 1


def normalize_down(x, gain_col, bias_col):
    average = jnp.mean(x, axis=0, keepdims=True)
    centred = x - average
    variance = jnp.mean(centred * centred, axis=0, keepdims=True)
    return centred * lax.rsqrt(variance + EPS) * gain_col + bias_col


def column(row, width):
    turned = jnp.broadcast_to(row, (LANES, row.shape[1])).T
    return jnp.concatenate([turned] * (width // LANES), axis=1)


def group_at(slot, groups):
    return lax.rem(slot + groups - lax.rem(lax.axis_index("col"), groups), groups)


def load_down(z_ref, chunk, groups):
    lane_rows = z_ref.shape[0] // groups
    columns = [
        jnp.concatenate(
            [
                z_ref[chunk * PER + q + lane_rows * group_at(slot, groups)]
                for slot in range(groups)
            ],
            axis=0,
        ).astype(jnp.float32).T
        for q in range(PER)
    ]
    return jnp.concatenate(columns, axis=1)


def stacked_weights(proj_ref, gate_ref, closer_ref, layer):
    half = jnp.asarray(0.5, jnp.bfloat16)
    return jnp.concatenate(
        [(ref[layer] * half).T for ref in (proj_ref, gate_ref, closer_ref)], axis=0
    )


def project_chunk(chunk, normed, mask, weights, scratch):
    product = jnp.dot(weights, normed.astype(jnp.bfloat16), preferred_element_type=jnp.float32)
    rows = (product.shape[0] - normed.shape[0]) // 2
    halves = double_sigmoid(product[rows : 2 * rows]) * (product[:rows] * mask)
    for q in range(PER):
        first = (chunk * PER + q) * (rows + PAD)
        scratch[first : first + rows, :] = halves[:, q * LANES : (q + 1) * LANES]
    return double_sigmoid(product[2 * rows :]).astype(jnp.bfloat16)


def spread_halves(scratch, halves_ref, devices):
    count, slots, lane_rows, _ = halves_ref.shape
    per_device = slots // 2
    hidden = count * per_device
    for d in devices:
        for slot in range(slots):
            h = (slot // per_device) * hidden + d * per_device + slot % per_device
            rows = scratch[pl.ds(h, lane_rows, stride=2 * hidden + PAD), :]
            halves_ref[d, slot] = rows.astype(jnp.bfloat16)


def slots_kernel(cols, slots_ref):
    slots_ref[...] = lax.broadcasted_iota(jnp.int32, slots_ref.shape, 1) // cols


def prepare_kernel(
    groups, rows, cols, slots_ref, gain_ref, bias_ref, proj_ref, gate_ref, mask_row_ref,
    closer_ref, out_gain_ref, out_bias_ref, final_ref,
    mask_ref, turned_ref, weights_ref, rows_ref, mask_col_ref,
):
    tokens = mask_row_ref.shape[1]
    lane_rows = rows // groups

    shift = lax.rem(tokens - lax.axis_index("col") * cols, tokens)
    mask_row = mask_row_ref[...].astype(jnp.float32)
    from_here = pltpu.roll(jnp.broadcast_to(mask_row, (8, tokens)), shift, 1)[:, :LANES]
    col_mask = from_here
    for slot in range(1, groups):
        col_mask = jnp.where(
            slots_ref[...] == slot, pltpu.roll(from_here, slot * cols, 1), col_mask
        )
    mask_col_ref[...] = column(mask_row, LANES)
    first_row = lax.axis_index("row") * rows
    for s in range(lane_rows):
        row_mask = jnp.zeros((1, LANES), jnp.float32)
        for slot in range(groups):
            row = first_row + s + lane_rows * group_at(slot, groups)
            row_mask = jnp.where(
                slots_ref[0:1, :] == slot, mask_col_ref[pl.ds(row, 1), :], row_mask
            )
        lanes = slice((s % PER) * LANES, (s % PER + 1) * LANES)
        mask_ref[s // PER, :, lanes] = row_mask * col_mask[0:1]

    half = jnp.asarray(0.5, jnp.bfloat16)
    turned_ref[0] = (final_ref[0] * half).T
    turned_ref[1] = (final_ref[1] * half).T
    for layer in range(2):
        weights_ref[layer] = stacked_weights(proj_ref, gate_ref, closer_ref, layer)
    table = [
        (out_gain_ref, 0), (out_bias_ref, 0), (gain_ref, 1), (bias_ref, 1), (out_gain_ref, 1),
        (out_bias_ref, 1), (gain_ref, 0), (bias_ref, 0),
    ]
    for n, (ref, layer) in enumerate(table):
        rows_ref[n : n + 1, :] = ref[layer : layer + 1, :]


def first_kernel(
    groups, z_ref, mask_ref, weights_ref, rows_ref, halves_ref, z_down_ref, closing_ref, scratch
):
    lane_rows = z_ref.shape[0] // groups
    weights = weights_ref[0]
    gain_col, bias_col = [column(rows_ref[n : n + 1, :], PER * LANES) for n in (6, 7)]
    for chunk in range(lane_rows // PER):
        z = load_down(z_ref, chunk, groups)
        z_down_ref[chunk] = z.astype(jnp.bfloat16)
        normed = normalize_down(z, gain_col, bias_col)
        closing_ref[chunk] = project_chunk(chunk, normed, mask_ref[chunk], weights, scratch)
    spread_halves(scratch, halves_ref, range(halves_ref.shape[0]))


def finish_chunk(chunk, lane_rows, sums_scratch, gain_col, bias_col, final, closing_ref, z_down_ref):
    hidden = final.shape[1]
    summed = jnp.concatenate(
        [
            sums_scratch[pl.ds(chunk * PER + q, hidden, stride=lane_rows + PAD), :]
            for q in range(PER)
        ],
        axis=1,
    )
    lifted = normalize_down(summed, gain_col, bias_col).astype(jnp.bfloat16)
    update = jnp.dot(final, lifted, preferred_element_type=jnp.float32)
    return (z_down_ref[chunk].astype(jnp.float32) + closing_ref[chunk].astype(jnp.float32) * update).astype(
        jnp.bfloat16
    )


def load_sums(sums_ref, scratch):
    devices, per_device, lane_rows, _ = sums_ref.shape
    for d in range(devices):
        for slot in range(per_device):
            first = (d * per_device + slot) * (lane_rows + PAD)
            scratch[first : first + lane_rows, :] = sums_ref[d, slot].astype(jnp.float32)


def middle_kernel(
    z_down_ref, sums_ref, closing_ref, turned_ref, weights_ref, rows_ref, mask_ref,
    halves_ref, z_out_ref, closing_out_ref, sums_scratch, scratch,
):
    lane_rows = sums_ref.shape[2]
    load_sums(sums_ref, sums_scratch)
    final = turned_ref[0]
    weights = weights_ref[1]
    out_gain_col, out_bias_col, gain_col, bias_col = [
        column(rows_ref[n : n + 1, :], PER * LANES) for n in range(4)
    ]
    for chunk in range(lane_rows // PER):
        z = finish_chunk(
            chunk, lane_rows, sums_scratch, out_gain_col, out_bias_col, final, closing_ref,
            z_down_ref,
        )
        z_out_ref[chunk] = z
        normed = normalize_down(z.astype(jnp.float32), gain_col, bias_col)
        closing_out_ref[chunk] = project_chunk(chunk, normed, mask_ref[chunk], weights, scratch)
    spread_halves(scratch, halves_ref, range(halves_ref.shape[0]))


def finish_kernel(
    groups, z_down_ref, sums_ref, closing_ref, turned_ref, rows_ref, out_hbm, sums_scratch, out_ref, out_sems,
):
    lane_rows = sums_ref.shape[2]
    cols = LANES // groups
    load_sums(sums_ref, sums_scratch)
    final = turned_ref[1]
    gain_col, bias_col = [column(rows_ref[n : n + 1, :], PER * LANES) for n in (4, 5)]
    copies = []
    for chunk in range(lane_rows // PER):
        z = finish_chunk(
            chunk, lane_rows, sums_scratch, gain_col, bias_col, final, closing_ref, z_down_ref
        ).astype(jnp.float32)
        half = PER // 2
        for first_q in range(0, PER, half):
            for q in range(first_q, first_q + half):
                part = z[:, q * LANES : (q + 1) * LANES].T.astype(jnp.bfloat16)
                for slot in range(groups):
                    row = chunk * PER + q + lane_rows * group_at(slot, groups)
                    out_ref[row] = part[slot * cols : (slot + 1) * cols]
            for slot in range(groups):
                row = chunk * PER + first_q + lane_rows * group_at(slot, groups)
                some = pl.ds(row, half)
                copy = pltpu.make_async_copy(
                    out_ref.at[some], out_hbm.at[some], out_sems.at[len(copies)]
                )
                copy.start()
                copies.append(copy)
    for copy in copies:
        copy.wait()


def triangle_kernel(
    layer, groups, mesh_rows, mesh_cols, halves_ref, sums_ref, left, right
):
    per_device = sums_ref.shape[1]
    lane_rows = sums_ref.shape[2]
    cols = LANES // groups
    lane_slot = lax.broadcasted_iota(jnp.int32, (1, LANES), 1) // cols

    def pick(pieces):
        out = pieces[0]
        for n in range(1, groups):
            out = jnp.where(lane_slot == n, pieces[n], out)
        return out

    def turned(value, slots):
        places = slots * cols % LANES
        return pltpu.roll(value, places, 1) if places else value

    def assemble(slot, target):
        for r in range(mesh_rows):
            for t in range(mesh_cols // groups):
                blocks = [
                    halves_ref[r * mesh_cols + t * groups + u, slot] for u in range(groups)
                ]
                for g in range(groups):
                    piece = turned(pick([blocks[(n - g) % groups] for n in range(groups)]), -g)
                    first = (r * groups + g) * lane_rows
                    target[first : first + lane_rows, t * LANES : (t + 1) * LANES] = piece

    for q in range(per_device):
        assemble(q, left.at[q])
        assemble(per_device + q, right.at[q])
        summed = lax.dot_general(
            left[q], right[q], NT if layer == 0 else TN, preferred_element_type=jnp.float32
        ).astype(jnp.bfloat16)
        for r in range(mesh_rows):
            for t in range(mesh_cols // groups):
                blocks = [
                    turned(
                        summed[
                            (r * groups + g) * lane_rows : (r * groups + g + 1) * lane_rows,
                            t * LANES : (t + 1) * LANES,
                        ],
                        g,
                    )
                    for g in range(groups)
                ]
                for u in range(groups):
                    piece = pick([blocks[(n - u) % groups] for n in range(groups)])
                    sums_ref[r * mesh_cols + t * groups + u, q] = piece


def vmem(count):
    return [pl.BlockSpec(memory_space=pltpu.VMEM)] * count


def by_channel(mesh_rows, mesh_cols, pair_map, token_mask, norm_gain, norm_bias, proj_weight,
               gate_weight, out_gain, out_bias, final_weight, output_gate):
    rows, cols, channels = pair_map.shape
    hidden = proj_weight.shape[2] // 2
    tokens = token_mask.shape[0]
    devices = mesh_rows * mesh_cols
    per_device = hidden // devices
    groups = LANES // cols
    lane_rows = rows // groups
    chunks = lane_rows // PER
    params = pltpu.CompilerParams(vmem_limit_bytes=40 * 1024 * 1024)
    halves_type = jax.ShapeDtypeStruct((devices, 2 * per_device, lane_rows, LANES), jnp.bfloat16)
    sums_type = jax.ShapeDtypeStruct((devices, per_device, lane_rows, LANES), jnp.bfloat16)
    down_type = jax.ShapeDtypeStruct((chunks, channels, PER * LANES), jnp.bfloat16)
    mask_type = jax.ShapeDtypeStruct((chunks, 1, PER * LANES), jnp.float32)
    halves_scratch = pltpu.VMEM(((lane_rows + 1) * (2 * hidden + PAD), LANES), jnp.float32)
    sums_scratch = pltpu.VMEM(((hidden + 1) * (lane_rows + PAD), LANES), jnp.float32)
    hbm = pl.BlockSpec(memory_space=pltpu.HBM)
    def exchange(value):
        return lax.all_to_all(value, ("row", "col"), split_axis=0, concat_axis=0, tiled=True)

    def triangle(layer, halves):
        return pl.pallas_call(
            functools.partial(triangle_kernel, layer, groups, mesh_rows, mesh_cols),
            out_shape=sums_type,
            in_specs=vmem(1),
            out_specs=pl.BlockSpec(memory_space=pltpu.VMEM),
            scratch_shapes=[pltpu.VMEM((per_device, tokens, tokens), jnp.bfloat16)] * 2,
            compiler_params=params,
        )(halves)

    slots = pl.pallas_call(
        functools.partial(slots_kernel, cols),
        out_shape=jax.ShapeDtypeStruct((8, LANES), jnp.int32),
        out_specs=pl.BlockSpec(memory_space=pltpu.VMEM),
        compiler_params=params,
        cost_estimate=pl.CostEstimate(
            flops=10**9, bytes_accessed=8 * LANES * 4, transcendentals=0
        ),
    )()
    mask, turned, weights, table = pl.pallas_call(
        functools.partial(prepare_kernel, groups, rows, cols),
        out_shape=(
            mask_type,
            jax.ShapeDtypeStruct((2, channels, hidden), jnp.bfloat16),
            jax.ShapeDtypeStruct((2, 4 * hidden + channels, channels), jnp.bfloat16),
            jax.ShapeDtypeStruct((8, channels), jnp.float32),
        ),
        in_specs=vmem(10),
        out_specs=tuple(vmem(4)),
        scratch_shapes=[pltpu.VMEM((tokens, LANES), jnp.float32)],
        compiler_params=params,
    )(slots, norm_gain, norm_bias, proj_weight, gate_weight, token_mask.reshape(1, tokens),
      output_gate, out_gain, out_bias, final_weight)
    halves, z_down, closing = pl.pallas_call(
        functools.partial(first_kernel, groups),
        out_shape=(halves_type, down_type, down_type),
        in_specs=vmem(4),
        out_specs=tuple(vmem(3)),
        scratch_shapes=[halves_scratch],
        compiler_params=params,
    )(pair_map, mask, weights, table)
    sums = exchange(triangle(0, exchange(halves)))
    halves, z_down, closing = pl.pallas_call(
        middle_kernel,
        out_shape=(halves_type, down_type, down_type),
        in_specs=vmem(7),
        out_specs=tuple(vmem(3)),
        scratch_shapes=[sums_scratch, halves_scratch],
        compiler_params=params,
    )(z_down, sums, closing, turned, weights, table, mask)
    sums = exchange(triangle(1, exchange(halves)))
    return pl.pallas_call(
        functools.partial(finish_kernel, groups),
        out_shape=jax.ShapeDtypeStruct(pair_map.shape, jnp.bfloat16),
        in_specs=vmem(5),
        out_specs=hbm,
        scratch_shapes=[
            sums_scratch,
            pltpu.VMEM(pair_map.shape, jnp.bfloat16),
            pltpu.SemaphoreType.DMA((2 * chunks * groups,)),
        ],
        compiler_params=params,
    )(z_down, sums, closing, turned, table)


def normalize(values, gain_vector, bias_vector):
    average = jnp.mean(values, axis=-1, keepdims=True)
    centred = values - average
    variance = jnp.mean(centred * centred, axis=-1, keepdims=True)
    return centred * lax.rsqrt(variance + EPS) * gain_vector + bias_vector


def project(
    pair_map, pair_mask, norm_gain, norm_bias, proj_weight, gate_weight, output_gate, layer_id
):
    normed = normalize(
        pair_map.astype(jnp.float32), norm_gain[layer_id], norm_bias[layer_id]
    ).astype(jnp.bfloat16)
    projected = jnp.dot(normed, proj_weight[layer_id], preferred_element_type=jnp.float32)
    gating = jnp.dot(normed, gate_weight[layer_id], preferred_element_type=jnp.float32)
    halves = (jax.nn.sigmoid(gating) * projected * pair_mask[..., None]).astype(jnp.bfloat16)
    closing = jax.nn.sigmoid(
        jnp.dot(normed, output_gate[layer_id], preferred_element_type=jnp.float32)
    )
    return (halves, closing)


def finish(pair_map, summed, closing, out_gain, out_bias, final_weight, layer_id):
    lifted = normalize(summed.astype(jnp.float32), out_gain[layer_id], out_bias[layer_id]).astype(
        jnp.bfloat16
    )
    update = closing * jnp.dot(lifted, final_weight[layer_id], preferred_element_type=jnp.float32)
    return (pair_map.astype(jnp.float32) + update).astype(jnp.bfloat16)


def by_block(pair_map, token_mask, norm_gain, norm_bias, proj_weight, gate_weight, out_gain,
             out_bias, final_weight, output_gate):
    rows_here = pair_map.shape[0]
    cols_here = pair_map.shape[1]
    hidden = proj_weight.shape[2] // 2
    row_mask = lax.dynamic_slice_in_dim(
        token_mask, lax.axis_index("row") * rows_here, rows_here
    ).astype(jnp.float32)
    col_mask = lax.dynamic_slice_in_dim(
        token_mask, lax.axis_index("col") * cols_here, cols_here
    ).astype(jnp.float32)
    pair_mask = row_mask[:, None] * col_mask[None, :]
    halves, closing = project(
        pair_map, pair_mask, norm_gain, norm_bias, proj_weight, gate_weight, output_gate, 0
    )
    left_side = halves[..., :hidden]
    right_side = halves[..., hidden:]
    right_rows = lax.all_gather(right_side, "row", axis=0, tiled=True)
    partial_value = jnp.einsum(
        "ikh,jkh->ijh", left_side, right_rows, preferred_element_type=jnp.float32
    )
    summed = lax.psum_scatter(partial_value, "col", scatter_dimension=1, tiled=True).astype(
        jnp.bfloat16
    )
    pair_map = finish(pair_map, summed, closing, out_gain, out_bias, final_weight, 0)
    halves, closing = project(
        pair_map, pair_mask, norm_gain, norm_bias, proj_weight, gate_weight, output_gate, 1
    )
    left_side = halves[..., :hidden]
    right_side = halves[..., hidden:]
    left_cols = lax.all_gather(left_side, "col", axis=1, tiled=True)
    partial_value = jnp.einsum(
        "kih,kjh->ijh", left_cols, right_side, preferred_element_type=jnp.float32
    )
    summed = lax.psum_scatter(partial_value, "row", scatter_dimension=0, tiled=True).astype(
        jnp.bfloat16
    )
    return finish(pair_map, summed, closing, out_gain, out_bias, final_weight, 1)


def solution(mesh):
    mesh_rows, mesh_cols = mesh.shape["row"], mesh.shape["col"]

    def shards(pair_map, token_mask, norm_gain, norm_bias, proj_weight, *rest):
        rows, cols, _ = pair_map.shape
        hidden = proj_weight.shape[2] // 2
        groups = max(LANES // cols, 1)
        fits = (
            hidden % (mesh_rows * mesh_cols) == 0
            and LANES % cols == 0
            and rows % (16 * groups) == 0
            and mesh_cols % groups == 0
        )
        args = (pair_map, token_mask, norm_gain, norm_bias, proj_weight, *rest)
        if fits:
            return by_channel(mesh_rows, mesh_cols, *args)
        return by_block(*args)

    return jax.shard_map(
        shards,
        mesh=mesh,
        in_specs=(P("row", "col", None), P(), P(), P(), P(), P(), P(), P(), P(), P()),
        out_specs=P("row", "col", None),
        check_vma=False,
    )
```
